512 devices in a mesh: dp: 8 (over y), ctx: 64 (over z, x, core).
Axes of the slice: x: 4, y: 8, z: 8, core: 2. Of those that a mesh axis runs over, the one named last changes fastest.
Arguments:
- queries: bfloat16 [8, 8192, 512], P('dp', 'ctx'), may hold values from -4 to 4
- keys: bfloat16 [8, 8192, 512], P('dp', 'ctx'), may hold values from -4 to 4
- values: bfloat16 [8, 8192, 512], P('dp', 'ctx'), may hold values from -6 to 6
- upstream: bfloat16 [8, 8192, 512], P('dp', 'ctx'), may hold values from -6 to 6
- query_map: bfloat16 [8, 64, 64], replicated, may hold values from -0.75 to 0.75
- key_map: bfloat16 [8, 64, 64], replicated, may hold values from -0.75 to 0.75
Outputs:
- grad_queries: bfloat16 [8, 8192, 512], P('dp', 'ctx')
- grad_keys: bfloat16 [8, 8192, 512], P('dp', 'ctx')
- grad_values: bfloat16 [8, 8192, 512], P('dp', 'ctx')
- grad_query_map: bfloat16 [8, 64, 64], replicated
- grad_key_map: bfloat16 [8, 64, 64], replicated
The draws below stay inside these ranges and needn't reach their ends.
All inputs are finite; a program needn't handle non-finite values.
Results may differ from the reference program's by a relative error of at most 0.0015.
Values sent between devices are 32-bit elements; how exact they have to be, the bound alone decides.
No kernel may reach another device: no remote copies, remote signals or barrier semaphores. Data moves between devices by JAX's collectives and lax.ppermute only.
A program may use at most 64 MiB of HBM per device.

```python
import jax
import jax.numpy as jnp
from jax import lax

HEADS = 8
HEAD_DIM = 64
TOK_DEV = 128
SEQ = 8192
BATCH = 8
ALL_TOKENS = 65536
N_CTX = 64


def levels(key, dims, pieces, low, largest):
    def one(dim, blocks):
        draws = jax.random.uniform(jax.random.fold_in(jax.random.fold_in(key, 6), dim), (blocks,), jnp.float32, low / len(pieces), largest / len(pieces))
        return jnp.repeat(jnp.exp(draws), dims[dim] // blocks).reshape((-1,) + (1,) * (len(dims) - dim - 1))

    level = one(*pieces[0])
    for cut in pieces[1:]:
        level = level * one(*cut)
    return level


def noise(stream_key, dims, spread, reach, split=(), dtype=jnp.bfloat16):
    factor_of = levels(stream_key, dims, split, -0.22, 0.18) if split else 1.0
    result = jax.random.normal(stream_key, dims, jnp.float32) * spread * factor_of
    return jnp.minimum(jnp.maximum(result, -reach), reach).astype(dtype)


def setup_inputs(seed: int = 0) -> dict:
    splits = jax.random.split(jax.random.key(seed), 7)
    queries = noise(splits[0], (BATCH, SEQ, HEADS * HEAD_DIM), 1.0, 4.0, ((0, 8), (1, 64)))
    keys = noise(splits[1], (BATCH, SEQ, HEADS * HEAD_DIM), 1.0, 4.0, ((0, 8), (1, 64)))
    values = noise(splits[2], (BATCH, SEQ, HEADS * HEAD_DIM), 1.0, 6.0, ((0, 8), (1, 64)))
    upstream = noise(splits[3], (BATCH, SEQ, HEADS * HEAD_DIM), 1.0, 6.0, ((0, 8), (1, 64)))
    query_map = noise(splits[4], (HEADS, HEAD_DIM, HEAD_DIM), HEAD_DIM ** -0.5, 0.75)
    key_map = noise(splits[5], (HEADS, HEAD_DIM, HEAD_DIM), HEAD_DIM ** -0.5, 0.75)
    return {"queries": queries, "keys": keys, "values": values, "upstream": upstream, "query_map": query_map, "key_map": key_map}


def feature(z):
    up = jnp.exp(z)
    down = jnp.exp(-z)
    return jnp.concatenate([up / jnp.sum(up, -1, keepdims=True), down / jnp.sum(down, -1, keepdims=True)], -1)


def feature_back(z, grad):
    width = z.shape[-1]
    up = jnp.exp(z)
    down = jnp.exp(-z)
    plus = up / jnp.sum(up, -1, keepdims=True)
    minus = down / jnp.sum(down, -1, keepdims=True)
    first = grad[..., :width]
    second = grad[..., width:]
    return plus * (first - jnp.sum(plus * first, -1, keepdims=True)) - minus * (second - jnp.sum(minus * second, -1, keepdims=True))


def to_blocks(x):
    return jnp.transpose(x.reshape(HEADS, N_CTX, TOK_DEV, x.shape[-1]), (1, 0, 2, 3))


def from_blocks(x):
    return jnp.transpose(x, (1, 0, 2, 3)).reshape(HEADS, SEQ, x.shape[-1])


def one_sequence(items):
    query_seq, key_seq, value_seq, grad_seq, qmap, kmap = items
    hp = lax.Precision.HIGHEST
    qh = query_seq.reshape(SEQ, HEADS, HEAD_DIM).astype(jnp.float32)
    kh = key_seq.reshape(SEQ, HEADS, HEAD_DIM).astype(jnp.float32)
    vh = jnp.transpose(value_seq.reshape(SEQ, HEADS, HEAD_DIM).astype(jnp.float32), (1, 0, 2))
    gh = jnp.transpose(grad_seq.reshape(SEQ, HEADS, HEAD_DIM).astype(jnp.float32), (1, 0, 2))
    zq = jnp.einsum('thd,hde->hte', qh, qmap, precision=hp)
    zk = jnp.einsum('thd,hde->hte', kh, kmap, precision=hp)
    qf = to_blocks(feature(zq))
    kf = to_blocks(feature(zk))
    vb = to_blocks(vh)
    gb = to_blocks(gh)
    mask = jnp.tril(jnp.ones((TOK_DEV, TOK_DEV), jnp.float32))
    local_kv = jnp.einsum('bhtf,bhte->bhfe', kf, vb, precision=hp)
    local_ks = jnp.sum(kf, 2)
    state = jnp.cumsum(local_kv, 0) - local_kv
    ksum = jnp.cumsum(local_ks, 0) - local_ks
    scores = jnp.einsum('bhtf,bhsf->bhts', qf, kf, precision=hp) * mask
    numer = jnp.einsum('bhtf,bhfe->bhte', qf, state, precision=hp) + jnp.einsum('bhts,bhse->bhte', scores, vb, precision=hp)
    denom = jnp.einsum('bhtf,bhf->bht', qf, ksum, precision=hp) + jnp.sum(scores, -1)
    attended = numer / denom[..., None]
    dnum = gb / denom[..., None]
    dden = -jnp.sum(gb * attended, -1) / denom
    local_ds = jnp.einsum('bhtf,bhte->bhfe', qf, dnum, precision=hp)
    local_dz = jnp.einsum('bhtf,bht->bhf', qf, dden, precision=hp)
    later_ds = jnp.cumsum(local_ds[::-1], 0)[::-1] - local_ds
    later_dz = jnp.cumsum(local_dz[::-1], 0)[::-1] - local_dz
    mixing = mask * (jnp.einsum('bhte,bhse->bhts', dnum, vb, precision=hp) + dden[..., None])
    grad_qf = jnp.einsum('bhte,bhfe->bhtf', dnum, state, precision=hp) + dden[..., None] * ksum[:, :, None, :] + jnp.einsum('bhts,bhsf->bhtf', mixing, kf, precision=hp)
    grad_kf = jnp.einsum('bhts,bhtf->bhsf', mixing, qf, precision=hp) + jnp.einsum('bhse,bhfe->bhsf', vb, later_ds, precision=hp) + later_dz[:, :, None, :]
    grad_v = jnp.einsum('bhts,bhte->bhse', scores, dnum, precision=hp) + jnp.einsum('bhsf,bhfe->bhse', kf, later_ds, precision=hp)
    dzq = feature_back(zq, from_blocks(grad_qf))
    dzk = feature_back(zk, from_blocks(grad_kf))
    grad_q = jnp.einsum('hte,hde->thd', dzq, qmap, precision=hp).reshape(SEQ, HEADS * HEAD_DIM)
    grad_k = jnp.einsum('hte,hde->thd', dzk, kmap, precision=hp).reshape(SEQ, HEADS * HEAD_DIM)
    grad_vv = jnp.transpose(from_blocks(grad_v), (1, 0, 2)).reshape(SEQ, HEADS * HEAD_DIM)
    gq = jnp.einsum('thd,hte->hde', qh, dzq, precision=hp)
    gk = jnp.einsum('thd,hte->hde', kh, dzk, precision=hp)
    return grad_q.astype(jnp.bfloat16), grad_k.astype(jnp.bfloat16), grad_vv.astype(jnp.bfloat16), gq, gk


def reference(queries, keys, values, upstream, query_map, key_map):
    qmap = query_map.astype(jnp.float32)
    kmap = key_map.astype(jnp.float32)
    count = queries.shape[0]
    qmaps = jnp.broadcast_to(qmap, (count,) + qmap.shape)
    kmaps = jnp.broadcast_to(kmap, (count,) + kmap.shape)
    grad_q, grad_k, grad_v, gq, gk = lax.map(one_sequence, (queries, keys, values, upstream, qmaps, kmaps))
    scale = float(ALL_TOKENS) ** -0.5
    return grad_q, grad_k, grad_v, (jnp.sum(gq, 0) * scale).astype(jnp.bfloat16), (jnp.sum(gk, 0) * scale).astype(jnp.bfloat16)
```

```python
import functools

import jax
import jax.numpy as jnp
import numpy as np
from jax import lax
from jax.experimental import pallas as pl
from jax.experimental.pallas import tpu as pltpu
from jax.sharding import Mesh, PartitionSpec as P

F32 = jnp.float32
BF16 = jnp.bfloat16
CTX = ("z", "x", "core")
CHIPS = ("z", "x")
LANES = 128
HALF = 64
TOK = 128
PAIRS = 4


def nn(a, b):
    return lax.dot_general(a, b, (((1,), (0,)), ((), ())), preferred_element_type=F32)


def nt(a, b):
    return lax.dot_general(a, b, (((1,), (1,)), ((), ())), preferred_element_type=F32)


def split(x):
    hi = x.astype(BF16)
    return hi, (x - hi.astype(F32)).astype(BF16)


def both(op, a, w):
    rows = a[0].shape[0]
    out = op(jnp.concatenate(a, 0), w)
    return out[:rows] + out[rows:]


def three(op, a, b):
    return both(op, a, b[0]) + op(a[0], b[1])


def iota(shape, dim):
    return lax.broadcasted_iota(jnp.int32, shape, dim)


def low_lane(shape):
    return lax.rem(iota(shape, 1), LANES) < HALF


def diagonal(shape):
    return (lax.rem(iota(shape, 0), LANES) < HALF) == low_lane(shape)


def swap(x):
    return jnp.concatenate([x[HALF:], x[:HALF]], 0)


def pack(d):
    return jnp.where(diagonal((LANES, LANES)), d[:, :LANES], swap(d[:, LANES:]))


def unpack(x):
    diag = diagonal((LANES, LANES))
    return jnp.concatenate([jnp.where(diag, x, 0.0), jnp.where(diag, swap(x), 0.0)], 1)


def stacked(x):
    low = low_lane(x.shape)
    zero = jnp.zeros_like(x)
    return jnp.concatenate([jnp.where(low, x, zero), jnp.where(low, zero, x)], 0)


def side_by_side(x):
    return jnp.concatenate([x[:TOK], x[TOK:]], 1)


def block_ones():
    return jnp.where(diagonal((LANES, LANES)), 1.0, 0.0).astype(BF16)


def head_sum(x):
    return both(nn, split(x), block_ones())


def block_maps(maps_ref):
    twice = jnp.where(
        iota((HALF, LANES), 0) == lax.rem(iota((HALF, LANES), 1), HALF), 1.0, 0.0
    ).astype(BF16)
    wide = nn(maps_ref[...], twice)
    return jnp.where(diagonal(wide.shape), wide, 0.0).astype(BF16)


def cols(p, width=LANES):
    return slice(p * width, (p + 1) * width)


def softmaxes(z):
    low = low_lane(z.shape)
    inf = jnp.inf
    top = jnp.where(
        low,
        jnp.max(jnp.where(low, z, -inf), 1, keepdims=True),
        jnp.max(jnp.where(low, -inf, z), 1, keepdims=True),
    )
    bottom = jnp.where(
        low,
        jnp.min(jnp.where(low, z, inf), 1, keepdims=True),
        jnp.min(jnp.where(low, inf, z), 1, keepdims=True),
    )
    up = jnp.exp(z - top)
    down = jnp.exp(bottom - z)
    return up / head_sum(up), down / head_sum(down)


def chip_index(axis_sizes):
    return lax.axis_index("z") * axis_sizes["x"] + lax.axis_index("x"), lax.axis_index("core")


def features_kernel(q, k, v, qmap, kmap, send, kv, qh, ql, kh, kl):
    wq = block_maps(qmap)
    wk = block_maps(kmap)
    sums_p, sums_m = [], []
    chips = send.shape[0]
    for p in range(PAIRS):
        c = cols(p)
        pk, mk = softmaxes(nn(k[:, c], wk[c]))
        sums_p.append(jnp.sum(pk, 0, keepdims=True))
        sums_m.append(jnp.sum(mk, 0, keepdims=True))
        hi, lo = split(jnp.concatenate([pk, mk], 1))
        kh[:, cols(p, 2 * LANES)] = hi
        kl[:, cols(p, 2 * LANES)] = lo
        vt = v[:, c].T
        kv[c, :] = pack(nn(vt, hi) + nn(vt, lo))
    send[:, : 4 * LANES // chips, :] = kv[...].reshape(chips, 4 * LANES // chips, LANES)
    sums = jnp.concatenate(sums_p + sums_m, 0)
    send[:, 4 * LANES // chips :, :] = jnp.broadcast_to(sums[None], (chips, 8, LANES))
    for p in range(PAIRS):
        c = cols(p)
        pq, mq = softmaxes(nn(q[:, c], wq[c]))
        hi, lo = split(jnp.concatenate([pq, mq], 1))
        qh[:, cols(p, 2 * LANES)] = hi
        ql[:, cols(p, 2 * LANES)] = lo


def local_kernel(v, qh, ql, kh, kl, num, den, sth, stl):
    row = lax.rem(iota((2 * TOK, TOK), 0), TOK)
    lane = iota((2 * TOK, TOK), 1)
    for p in range(PAIRS):
        w = cols(p, 2 * LANES)
        q2 = (qh[:, w], ql[:, w])
        k2 = (kh[:, w], kl[:, w])
        scores = three(nt, (stacked(q2[0]), stacked(q2[1])), k2)
        scores = side_by_side(jnp.where(lane <= row, scores, 0.0))
        v2 = stacked(v[:, cols(p)])
        ones = stacked(jnp.ones((TOK, LANES), BF16))
        out = both(nn, split(scores), jnp.concatenate([v2, ones], 1))
        num[:, cols(p)] = out[:, :LANES]
        den[:, cols(p)] = out[:, LANES:]
        back = three(nt, (stacked(k2[0]), stacked(k2[1])), q2)
        hi, lo = split(side_by_side(jnp.where(lane >= row, back, 0.0)))
        sth[:, w] = hi
        stl[:, w] = lo


def second_kernel(sizes, got, g, qh, ql, denl, send, den, dn, ds, ksum):
    chip, core = chip_index(sizes)
    chips = send.shape[0]
    rows = 4 * LANES // chips
    part = rows // 2
    start = pl.multiple_of(core * part, part)
    acc = jnp.zeros((8, LANES), F32)
    run = jnp.zeros((part, LANES), F32)
    for m in range(chips):
        send[m, :part, :] = run
        run = run + (got[0, m, pl.ds(start, part), :] + got[1, m, pl.ds(start, part), :])
        zero = got[0, m, rows:, :]
        one = got[1, m, rows:, :]
        acc = acc + jnp.where(
            m < chip, zero + one, jnp.where((m == chip) & (core == 1), zero, 0.0)
        )
    ksum[...] = acc
    diag = diagonal((LANES, 2 * LANES))
    for p in range(PAIRS):
        c = cols(p)
        w = cols(p, 2 * LANES)
        q2 = (qh[:, w], ql[:, w])
        sums = jnp.concatenate([acc[p : p + 1], acc[p + 4 : p + 5]], 1)
        sums = jnp.where(diag, jnp.broadcast_to(sums, (LANES, 2 * LANES)), 0.0)
        d = denl[:, c] + three(nt, q2, split(sums))
        den[:, c] = d
        scaled = g[:, c].astype(F32) / d
        dn[:, c] = scaled
        ds[c, :] = pack(three(nn, split(scaled.T), q2))
    send[:, part:, :] = ds[...].reshape(chips, rows, LANES)


def gathered(got, part):
    return jnp.stack([got[0, :, :part, :], got[1, :, :part, :]], 1).reshape(4 * LANES, LANES)


def third_kernel(sizes, got, kvs, g, qh, ql, numl, den, send, dd, state):
    _, core = chip_index(sizes)
    chips = send.shape[0]
    rows = 4 * LANES // chips
    part = rows // 2
    start = pl.multiple_of(part + core * part, part)
    run = jnp.zeros((part, LANES), F32)
    for m in reversed(range(chips)):
        send[m, :part, :] = run
        run = run + (got[0, m, pl.ds(start, part), :] + got[1, m, pl.ds(start, part), :])
    whole = gathered(got, part) + jnp.where(core == 1, kvs[0], 0.0)
    state[...] = whole
    sums_p, sums_m = [], []
    for p in range(PAIRS):
        c = cols(p)
        w = cols(p, 2 * LANES)
        q2 = (qh[:, w], ql[:, w])
        numer = numl[:, c] + three(nt, q2, split(unpack(whole[c])))
        d = den[:, c]
        dden = -head_sum(g[:, c].astype(F32) * (numer / d)) / d
        dd[:, c] = dden
        full = q2[0].astype(F32) + q2[1].astype(F32)
        sums_p.append(jnp.sum(full[:, :LANES] * dden, 0, keepdims=True))
        sums_m.append(jnp.sum(full[:, LANES:] * dden, 0, keepdims=True))
    sums = jnp.concatenate(sums_p + sums_m, 0)
    send[:, part:, :] = jnp.broadcast_to(sums[None], (chips, 8, LANES))


def feature_back(f2, grad):
    full = f2[0].astype(F32) + f2[1].astype(F32)
    plus, minus = full[:, :LANES], full[:, LANES:]
    first, second = grad[:, :LANES], grad[:, LANES:]
    return plus * (first - head_sum(plus * first)) - minus * (second - head_sum(minus * second))


def one_hot_lane(shape):
    return lax.rem(iota(shape, 1), HALF) == 0


def fourth_kernel(
    q, v, qmap, qh, ql, kh, kl, sth, stl, dn, dd, state, ksum, gq_out, gq_map, gkl, gvl
):
    wq = block_maps(qmap)
    row = lax.rem(iota((2 * TOK, TOK), 0), TOK)
    lane = iota((2 * TOK, TOK), 1)
    hot = one_hot_lane((TOK, LANES))
    for p in range(PAIRS):
        c = cols(p)
        w = cols(p, 2 * LANES)
        q2 = (qh[:, w], ql[:, w])
        k2 = (kh[:, w], kl[:, w])
        v2 = v[:, c]
        scaled = dn[:, c]
        dden = dd[:, c]
        s2 = split(scaled)
        wide = split(jnp.concatenate([scaled, jnp.where(hot, dden, 0.0)], 1))
        ones = jnp.ones((TOK, LANES), BF16)
        mixing = both(
            nt, (stacked(wide[0]), stacked(wide[1])), jnp.concatenate([v2, ones], 1)
        )
        mixing = split(side_by_side(jnp.where(lane <= row, mixing, 0.0)))
        grad = three(nn, mixing, (stacked(k2[0]), stacked(k2[1])))
        grad = grad + three(nn, s2, split(unpack(state[c, :])))
        grad = grad + jnp.concatenate(
            [dden * ksum[p : p + 1, :], dden * ksum[p + 4 : p + 5, :]], 1
        )
        dzq = feature_back(q2, grad)
        z2 = split(dzq)
        gq_out[:, c] = both(nt, z2, wq[c]).astype(BF16)
        qt = q[:, c].T
        gq_map[c, :] = nn(qt, z2[0]) + nn(qt, z2[1])
        vwide = stacked(jnp.concatenate([v2, jnp.where(hot, 1.0, 0.0).astype(BF16)], 1))
        back = nt(vwide, wide[0]) + nt(vwide, wide[1])
        back = split(side_by_side(jnp.where(lane >= row, back, 0.0)))
        gkl[:, w] = three(nn, back, (stacked(q2[0]), stacked(q2[1])))
        gvl[:, c] = three(nn, (sth[:, w], stl[:, w]), (stacked(s2[0]), stacked(s2[1])))


def fifth_kernel(sizes, got, dss, k, v, kh, kl, gkl, gq_map, send, dz, later):
    chip, core = chip_index(sizes)
    chips = send.shape[0]
    rows = 4 * LANES // chips
    part = rows // 2
    acc = jnp.zeros((8, LANES), F32)
    for m in range(chips):
        zero = got[0, m, part:, :]
        one = got[1, m, part:, :]
        acc = acc + jnp.where(
            m > chip, zero + one, jnp.where((m == chip) & (core == 0), one, 0.0)
        )
    whole = gathered(got, part) + jnp.where(core == 0, dss[1], 0.0)
    later[...] = whole
    out = []
    for p in range(PAIRS):
        c = cols(p)
        w = cols(p, 2 * LANES)
        k2 = (kh[:, w], kl[:, w])
        v2 = v[:, c]
        sums = jnp.concatenate([acc[p : p + 1], acc[p + 4 : p + 5]], 1)
        grad = gkl[:, w] + sums + nn(
            jnp.concatenate([v2, v2], 1), jnp.concatenate(split(unpack(whole[c])), 0)
        )
        dzk = feature_back(k2, grad)
        dz[:, c] = dzk
        z2 = split(dzk)
        kt = k[:, c].T
        out.append(
            pack(jnp.concatenate([gq_map[c, :], nn(kt, z2[0]) + nn(kt, z2[1])], 1))
        )
    send[...] = jnp.concatenate(out, 0).reshape(chips, rows, LANES)


def sixth_kernel(kmap, kh, kl, gvl, dz, later, gk_out, gv_out):
    wk = block_maps(kmap)
    for p in range(PAIRS):
        c = cols(p)
        w = cols(p, 2 * LANES)
        gk_out[:, c] = both(nt, split(dz[:, c]), wk[c]).astype(BF16)
        grad = gvl[:, c] + three(nt, (kh[:, w], kl[:, w]), split(unpack(later[c, :])))
        gv_out[:, c] = grad.astype(BF16)


def sum_kernel(got, send):
    total = got[0]
    for m in range(1, got.shape[0]):
        total = total + got[m]
    send[...] = jnp.broadcast_to(total[None], send.shape)


def last_kernel(scale, got, gq, gk):
    for p in range(PAIRS):
        x = got[cols(p), :] * scale
        y = pltpu.roll(x, HALF, 1)
        gq[2 * p] = x[:HALF, :HALF].astype(BF16)
        gq[2 * p + 1] = y[HALF:, :HALF].astype(BF16)
        gk[2 * p] = x[HALF:, :HALF].astype(BF16)
        gk[2 * p + 1] = y[:HALF, :HALF].astype(BF16)


def call(kernel, outs, *args, flops=10**8):
    shapes = [jax.ShapeDtypeStruct(shape, dtype) for shape, dtype in outs]
    moved = sum(a.size * a.dtype.itemsize for a in (*args, *shapes))
    return pl.pallas_call(
        kernel,
        out_shape=shapes,
        in_specs=[pl.BlockSpec(memory_space=pltpu.VMEM)] * len(args),
        out_specs=[pl.BlockSpec(memory_space=pltpu.VMEM)] * len(outs),
        compiler_params=pltpu.CompilerParams(vmem_limit_bytes=48 * 2**20),
        cost_estimate=pl.CostEstimate(flops=flops, bytes_accessed=moved, transcendentals=0),
    )(*args)


def per_device(sizes, queries, keys, values, upstream, query_map, key_map):
    chips = sizes["z"] * sizes["x"]
    rows = 4 * LANES // chips
    part = rows // 2
    q, k, v, g = (a.reshape(TOK, 4 * LANES) for a in (queries, keys, values, upstream))
    qmap = query_map.reshape(8 * HALF, HALF)
    kmap = key_map.reshape(8 * HALF, HALF)
    feats = ((TOK, 8 * LANES), BF16)
    flat = ((TOK, 4 * LANES), F32)
    small = ((TOK, 4 * LANES), BF16)
    square = ((4 * LANES, LANES), F32)

    def exchange(a):
        return lax.all_gather(lax.all_to_all(a, CHIPS, 0, 0), "core")

    send, kv, qh, ql, kh, kl = call(
        features_kernel,
        [((chips, rows + 8, LANES), F32), square, feats, feats, feats, feats],
        q, k, v, qmap, kmap,
    )
    got = exchange(send)
    kvs = lax.all_gather(kv, "core")
    numl, denl, sth, stl = call(
        local_kernel, [flat, flat, feats, feats], v, qh, ql, kh, kl, flops=10**9
    )
    send, den, dn, ds, ksum = call(
        functools.partial(second_kernel, sizes),
        [((chips, part + rows, LANES), F32), flat, flat, square, ((8, LANES), F32)],
        got, g, qh, ql, denl,
    )
    got = exchange(send)
    dss = lax.all_gather(ds, "core")
    send, dd, state = call(
        functools.partial(third_kernel, sizes),
        [((chips, part + 8, LANES), F32), flat, square],
        got, kvs, g, qh, ql, numl, den,
    )
    got = exchange(send)
    grad_q, gq_map, gkl, gvl = call(
        fourth_kernel,
        [small, square, ((TOK, 8 * LANES), F32), flat],
        q, v, qmap, qh, ql, kh, kl, sth, stl, dn, dd, state, ksum,
        flops=10**9,
    )
    send, dz, later = call(
        functools.partial(fifth_kernel, sizes),
        [((chips, rows, LANES), F32), flat, square],
        got, dss, k, v, kh, kl, gkl, gq_map,
    )
    got = lax.all_to_all(send, CHIPS, 0, 0)
    grad_k, grad_v = call(
        sixth_kernel, [small, small], kmap, kh, kl, gvl, dz, later, flops=10**9
    )
    others = sizes["dp"] * sizes["core"]
    (send,) = call(sum_kernel, [((others, rows, LANES), F32)], got)
    got = lax.all_to_all(send, ("dp", "core"), 0, 0)
    (send,) = call(sum_kernel, [((chips, rows, LANES), F32)], got)
    got = lax.all_to_all(send, CHIPS, 0, 0)
    scale = float(TOK * chips * others) ** (-0.5)
    heads = ((8, HALF, HALF), BF16)
    total_q, total_k = call(
        functools.partial(last_kernel, scale), [heads, heads], got.reshape(4 * LANES, LANES)
    )
    shape = queries.shape
    return grad_q.reshape(shape), grad_k.reshape(shape), grad_v.reshape(shape), total_q, total_k


def physical(mesh):
    dp, ctx = mesh.devices.shape
    x = 4 if ctx % 8 == 0 and ctx > 8 else 2
    sizes = {"dp": dp, "z": ctx // (2 * x), "x": x, "core": 2}
    return Mesh(mesh.devices.reshape(tuple(sizes.values())), tuple(sizes)), sizes


def solution(mesh):
    inner, sizes = physical(mesh)
    tokens = P("dp", CTX, None)
    return jax.shard_map(
        functools.partial(per_device, sizes),
        mesh=inner,
        in_specs=(tokens,) * 4 + (P(), P()),
        out_specs=(tokens,) * 3 + (P(), P()),
        check_vma=False,
    )
```

```python
import functools

import jax
import jax.numpy as jnp
import numpy as np
from jax import lax
from jax.experimental import pallas as pl
from jax.experimental.pallas import tpu as pltpu
from jax.sharding import Mesh, PartitionSpec as P

F32 = jnp.float32
BF16 = jnp.bfloat16
CTX = ("z", "x", "core")
CHIPS = ("z", "x")
LANES = 128
HALF = 64
TOK = 128
BLOCK = 256
PAIRS = 2
WIDE = PAIRS * LANES


def nn(a, b):
    return lax.dot_general(a, b, (((1,), (0,)), ((), ())), preferred_element_type=F32)


def nt(a, b):
    return lax.dot_general(a, b, (((1,), (1,)), ((), ())), preferred_element_type=F32)


def split(x):
    hi = x.astype(BF16)
    return hi, (x - hi.astype(F32)).astype(BF16)


def both(op, a, w):
    rows = a[0].shape[0]
    out = op(jnp.concatenate(a, 0), w)
    return out[:rows] + out[rows:]


def three(op, a, b):
    return both(op, a, b[0]) + op(a[0], b[1])


def iota(shape, dim):
    return lax.broadcasted_iota(jnp.int32, shape, dim)


def low_lane(shape):
    return lax.rem(iota(shape, 1), LANES) < HALF


def diagonal(shape):
    return (lax.rem(iota(shape, 0), LANES) < HALF) == low_lane(shape)


def swap(x):
    return jnp.concatenate([x[HALF:], x[:HALF]], 0)


def pack(d):
    return jnp.where(diagonal((LANES, LANES)), d[:, :LANES], swap(d[:, LANES:]))


def unpack(x):
    diag = diagonal((LANES, LANES))
    return jnp.concatenate([jnp.where(diag, x, 0.0), jnp.where(diag, swap(x), 0.0)], 1)


def stacked(x):
    low = low_lane(x.shape)
    zero = jnp.zeros_like(x)
    return jnp.concatenate([jnp.where(low, x, zero), jnp.where(low, zero, x)], 0)


def side_by_side(x):
    return jnp.concatenate([x[:BLOCK], x[BLOCK:]], 1)


def block_ones():
    return jnp.where(diagonal((LANES, LANES)), 1.0, 0.0).astype(BF16)


def head_sum(x):
    return both(nn, split(x), block_ones())


def block_maps(maps_ref):
    twice = jnp.where(
        iota((HALF, LANES), 0) == lax.rem(iota((HALF, LANES), 1), HALF), 1.0, 0.0
    ).astype(BF16)
    wide = nn(maps_ref[...], twice)
    return jnp.where(diagonal(wide.shape), wide, 0.0).astype(BF16)


def cols(p, width=LANES):
    return slice(p * width, (p + 1) * width)


def softmaxes(z):
    low = low_lane(z.shape)
    inf = jnp.inf
    top = jnp.where(
        low,
        jnp.max(jnp.where(low, z, -inf), 1, keepdims=True),
        jnp.max(jnp.where(low, -inf, z), 1, keepdims=True),
    )
    bottom = jnp.where(
        low,
        jnp.min(jnp.where(low, z, inf), 1, keepdims=True),
        jnp.min(jnp.where(low, inf, z), 1, keepdims=True),
    )
    up = jnp.exp(z - top)
    down = jnp.exp(bottom - z)
    return up / head_sum(up), down / head_sum(down)


def core():
    return lax.axis_index("core")


def chip(sizes):
    return lax.axis_index("z") * sizes["x"] + lax.axis_index("x")


def causal(rows):
    return iota((rows, BLOCK), 1) <= lax.rem(iota((rows, BLOCK), 0), BLOCK)


def causal_back(rows):
    return iota((rows, BLOCK), 1) >= lax.rem(iota((rows, BLOCK), 0), BLOCK)


def start_kernel(a, b, maps, send, own, wide, other, few, sems):
    mine = pl.ds(pl.multiple_of(core() * WIDE, WIDE), WIDE)
    theirs = pl.ds(pl.multiple_of((1 - core()) * WIDE, WIDE), WIDE)
    copies = []
    for i, ref in enumerate((a, b)):
        here = pl.ds(i * WIDE, WIDE)
        copies.append(pltpu.make_async_copy(ref.at[:, theirs], other.at[:, here], sems.at[2 * i]))
        copies.append(pltpu.make_async_copy(ref.at[:, mine], own.at[:, here], sems.at[2 * i + 1]))
    copies.append(pltpu.make_async_copy(maps.at[mine, :], few, sems.at[4]))
    for copy in copies:
        copy.start()
    copies[4].wait()
    wide[...] = block_maps(few)
    for copy in copies[:4]:
        copy.wait()
    send[...] = other[...].astype(F32)


def assemble(own, got, first, second):
    here = pl.ds(pl.multiple_of(core() * TOK, TOK), TOK)
    there = pl.ds(pl.multiple_of((1 - core()) * TOK, TOK), TOK)
    for i, ref in enumerate((first, second)):
        lanes = slice(i * WIDE, (i + 1) * WIDE)
        ref[here, :] = own[:, lanes]
        ref[there, :] = got[1 - core(), :, lanes].astype(BF16)


def keys_kernel(own, got, wk, send, k, v, kh, kl):
    assemble(own, got, k, v)
    chips = send.shape[0]
    rows = WIDE // chips
    state, sums_p, sums_m = [], [], []
    for p in range(PAIRS):
        c = cols(p)
        pk, mk = softmaxes(nn(k[:, c], wk[c]))
        sums_p.append(jnp.sum(pk, 0, keepdims=True))
        sums_m.append(jnp.sum(mk, 0, keepdims=True))
        hi, lo = split(jnp.concatenate([pk, mk], 1))
        kh[:, cols(p, 2 * LANES)] = hi
        kl[:, cols(p, 2 * LANES)] = lo
        vt = v[:, c].T
        state.append(pack(nn(vt, hi) + nn(vt, lo)))
    send[:, :rows, :] = jnp.concatenate(state, 0).reshape(chips, rows, LANES)
    sums = jnp.concatenate(sums_p + sums_m + [jnp.zeros((4, LANES), F32)], 0)
    send[:, rows:, :] = jnp.broadcast_to(sums[None], (chips, 8, LANES))


def queries_kernel(own, got, wq, v, kh, kl, q, g, qh, ql, num, den, sth, stl, cumk):
    assemble(own, got, q, g)
    mask = causal(2 * BLOCK)
    back_mask = causal_back(2 * BLOCK)
    tri = jnp.where(causal(BLOCK), 1.0, 0.0).astype(BF16)
    for p in range(PAIRS):
        c = cols(p)
        w = cols(p, 2 * LANES)
        pq, mq = softmaxes(nn(q[:, c], wq[c]))
        q2 = split(jnp.concatenate([pq, mq], 1))
        qh[:, w], ql[:, w] = q2
        k2 = (kh[:, w], kl[:, w])
        cumk[:, w] = nn(tri, k2[0]) + nn(tri, k2[1])
        scores = three(nt, (stacked(q2[0]), stacked(q2[1])), k2)
        scores = side_by_side(jnp.where(mask, scores, 0.0))
        v2 = stacked(v[:, c])
        ones = stacked(jnp.ones((BLOCK, LANES), BF16))
        out = both(nn, split(scores), jnp.concatenate([v2, ones], 1))
        num[:, c] = out[:, :LANES]
        den[:, c] = out[:, LANES:]
        back = three(nt, (stacked(k2[0]), stacked(k2[1])), q2)
        hi, lo = split(side_by_side(jnp.where(back_mask, back, 0.0)))
        both_heads = cols(p, 2 * BLOCK)
        sth[:, both_heads] = hi
        stl[:, both_heads] = lo


def second_kernel(sizes, got, g, qh, ql, denl, send, den, dn, ksum):
    chips = send.shape[0]
    rows = WIDE // chips
    me = chip(sizes)
    acc = jnp.zeros((8, LANES), F32)
    run = jnp.zeros((rows, LANES), F32)
    for m in range(chips):
        send[m, :rows, :] = run
        run = run + got[m, :rows, :]
        acc = acc + jnp.where(m < me, got[m, rows:, :], 0.0)
    ksum[...] = acc
    diag = diagonal((LANES, 2 * LANES))
    out = []
    for p in range(PAIRS):
        c = cols(p)
        w = cols(p, 2 * LANES)
        q2 = (qh[:, w], ql[:, w])
        sums = jnp.concatenate([acc[p : p + 1], acc[p + PAIRS : p + PAIRS + 1]], 1)
        sums = jnp.where(diag, jnp.broadcast_to(sums, (LANES, 2 * LANES)), 0.0)
        d = denl[:, c] + three(nt, q2, split(sums))
        den[:, c] = d
        scaled = g[:, c].astype(F32) / d
        dn[:, c] = scaled
        out.append(pack(three(nn, split(scaled.T), q2)))
    send[:, rows:, :] = jnp.concatenate(out, 0).reshape(chips, rows, LANES)


def local_kernel(v, qh, ql, kh, kl, sth, stl, dn, gql, gkl, gvl):
    mask = causal(2 * BLOCK)
    back_mask = causal_back(2 * BLOCK)
    for p in range(PAIRS):
        c = cols(p)
        w = cols(p, 2 * LANES)
        both_heads = cols(p, 2 * BLOCK)
        q2 = (qh[:, w], ql[:, w])
        k2 = (kh[:, w], kl[:, w])
        v2 = v[:, c]
        s2 = split(dn[:, c])
        d2 = (stacked(s2[0]), stacked(s2[1]))
        mixing = split(side_by_side(jnp.where(mask, both(nt, d2, v2), 0.0)))
        gql[:, w] = three(nn, mixing, (stacked(k2[0]), stacked(k2[1])))
        vv = stacked(v2)
        back = jnp.where(back_mask, nt(vv, s2[0]) + nt(vv, s2[1]), 0.0)
        back = split(side_by_side(back))
        gkl[:, w] = three(nn, back, (stacked(q2[0]), stacked(q2[1])))
        gvl[:, c] = three(nn, (sth[:, both_heads], stl[:, both_heads]), d2)


def third_kernel(got, g, qh, ql, numl, den, send, dd):
    chips = send.shape[0]
    rows = WIDE // chips
    run = jnp.zeros((rows, LANES), F32)
    for m in reversed(range(chips)):
        send[m, :rows, :] = run
        run = run + got[m, rows:, :]
    state = got[:, :rows, :].reshape(WIDE, LANES)
    sums_p, sums_m = [], []
    for p in range(PAIRS):
        c = cols(p)
        w = cols(p, 2 * LANES)
        q2 = (qh[:, w], ql[:, w])
        numer = numl[:, c] + three(nt, q2, split(unpack(state[c])))
        d = den[:, c]
        dden = -head_sum(g[:, c].astype(F32) * (numer / d)) / d
        dd[:, c] = dden
        full = q2[0].astype(F32) + q2[1].astype(F32)
        sums_p.append(jnp.sum(full[:, :LANES] * dden, 0, keepdims=True))
        sums_m.append(jnp.sum(full[:, LANES:] * dden, 0, keepdims=True))
    sums = jnp.concatenate(sums_p + sums_m + [jnp.zeros((4, LANES), F32)], 0)
    send[:, rows:, :] = jnp.broadcast_to(sums[None], (chips, 8, LANES))


def feature_back(f2, grad):
    full = f2[0].astype(F32) + f2[1].astype(F32)
    plus, minus = full[:, :LANES], full[:, LANES:]
    first, second = grad[:, :LANES], grad[:, LANES:]
    return plus * (first - head_sum(plus * first)) - minus * (second - head_sum(minus * second))


def twice(x):
    return jnp.concatenate([x, x], 1)


def fourth_kernel(got, q, wq, qh, ql, dn, dd, ksum, cumk, gql, gkl, whole, gq_map, gk_all):
    rows = WIDE // got.shape[0]
    state = got[:, :rows, :].reshape(WIDE, LANES)
    tri = jnp.where(causal_back(BLOCK), 1.0, 0.0).astype(BF16)
    for p in range(PAIRS):
        c = cols(p)
        w = cols(p, 2 * LANES)
        q2 = (qh[:, w], ql[:, w])
        dden = twice(dd[:, c])
        sums = jnp.concatenate([ksum[p : p + 1, :], ksum[p + PAIRS : p + PAIRS + 1, :]], 1)
        grad = gql[:, w] + three(nn, split(dn[:, c]), split(unpack(state[c])))
        grad = grad + dden * (sums + cumk[:, w])
        dzq = feature_back(q2, grad)
        z2 = split(dzq)
        whole[:, c] = both(nt, z2, wq[c])
        qt = q[:, c].T
        gq_map[c, :] = nn(qt, z2[0]) + nn(qt, z2[1])
        later = split((q2[0].astype(F32) + q2[1].astype(F32)) * dden)
        gk_all[:, w] = gkl[:, w] + nn(tri, later[0]) + nn(tri, later[1])


def fifth_kernel(sizes, got, k, v, kh, kl, gkl, gq_map, send, dz):
    chips = send.shape[0]
    rows = WIDE // chips
    me = chip(sizes)
    acc = jnp.zeros((8, LANES), F32)
    for m in range(chips):
        acc = acc + jnp.where(m > me, got[m, rows:, :], 0.0)
    later = got[:, :rows, :].reshape(WIDE, LANES)
    out = []
    for p in range(PAIRS):
        c = cols(p)
        w = cols(p, 2 * LANES)
        k2 = (kh[:, w], kl[:, w])
        sums = jnp.concatenate([acc[p : p + 1], acc[p + PAIRS : p + PAIRS + 1]], 1)
        grad = gkl[:, w] + sums + nn(
            twice(v[:, c]), jnp.concatenate(split(unpack(later[c])), 0)
        )
        dzk = feature_back(k2, grad)
        dz[:, c] = dzk
        z2 = split(dzk)
        kt = k[:, c].T
        out.append(
            pack(jnp.concatenate([gq_map[c, :], nn(kt, z2[0]) + nn(kt, z2[1])], 1))
        )
    send[...] = jnp.concatenate(out, 0).reshape(chips, rows, LANES)


def sixth_kernel(got, wk, kh, kl, gvl, dz, whole):
    rows = WIDE // got.shape[0]
    later = got[:, :rows, :].reshape(WIDE, LANES)
    for p in range(PAIRS):
        c = cols(p)
        w = cols(p, 2 * LANES)
        whole[:, c] = both(nt, split(dz[:, c]), wk[c])
        grad = gvl[:, c] + three(nt, (kh[:, w], kl[:, w]), split(unpack(later[c])))
        whole[:, WIDE + p * LANES : WIDE + (p + 1) * LANES] = grad


def theirs_kernel(whole, send):
    send[...] = whole[pl.ds(pl.multiple_of((1 - core()) * TOK, TOK), TOK), :]


def finish_kernel(whole, got, *outs):
    own = whole[pl.ds(pl.multiple_of(core() * TOK, TOK), TOK), :]
    other = got[1 - core()]
    first = core() == 0
    for i, out in enumerate(outs):
        lanes = slice(i * WIDE, (i + 1) * WIDE)
        a, b = own[:, lanes], other[:, lanes]
        out[:, :WIDE] = jnp.where(first, a, b).astype(BF16)
        out[:, WIDE:] = jnp.where(first, b, a).astype(BF16)


def sum_kernel(got, send):
    total = got[0]
    for m in range(1, got.shape[0]):
        total = total + got[m]
    send[...] = jnp.broadcast_to(total[None], send.shape)


def last_kernel(scale, got, gq, gk):
    for p in range(2 * PAIRS):
        x = got[cols(p), :] * scale
        y = pltpu.roll(x, HALF, 1)
        gq[2 * p] = x[:HALF, :HALF].astype(BF16)
        gq[2 * p + 1] = y[HALF:, :HALF].astype(BF16)
        gk[2 * p] = x[HALF:, :HALF].astype(BF16)
        gk[2 * p + 1] = y[:HALF, :HALF].astype(BF16)


def call(kernel, outs, *args, flops=10**8, space=pltpu.VMEM, scratch=(), room=32):
    shapes = [jax.ShapeDtypeStruct(shape, dtype) for shape, dtype in outs]
    moved = sum(a.size * a.dtype.itemsize for a in (*args, *shapes))
    return pl.pallas_call(
        kernel,
        out_shape=shapes,
        in_specs=[pl.BlockSpec(memory_space=space)] * len(args),
        out_specs=[pl.BlockSpec(memory_space=pltpu.VMEM)] * len(outs),
        scratch_shapes=scratch,
        compiler_params=pltpu.CompilerParams(vmem_limit_bytes=room * 2**20),
        cost_estimate=pl.CostEstimate(flops=flops, bytes_accessed=moved, transcendentals=0),
    )(*args)


def per_device(sizes, queries, keys, values, upstream, query_map, key_map):
    chips = sizes["z"] * sizes["x"]
    rows = WIDE // chips
    q, k, v, g = (a.reshape(TOK, 2 * WIDE) for a in (queries, keys, values, upstream))
    qmap = query_map.reshape(2 * WIDE, HALF)
    kmap = key_map.reshape(2 * WIDE, HALF)
    feats = ((BLOCK, 2 * WIDE), BF16)
    feats32 = ((BLOCK, 2 * WIDE), F32)
    flat = ((BLOCK, WIDE), F32)
    small = ((BLOCK, WIDE), BF16)
    scores = ((BLOCK, 2 * PAIRS * BLOCK), BF16)
    sums = ((8, LANES), F32)

    def across(a):
        return lax.all_gather(a, "core")

    def exchange(a):
        return lax.all_to_all(a, CHIPS, 0, 0)

    def start(a, b, maps, room):
        send, own, wide = call(
            start_kernel,
            [((TOK, 2 * WIDE), F32), ((TOK, 2 * WIDE), BF16), ((WIDE, LANES), BF16)],
            a, b, maps,
            space=pl.ANY,
            room=room,
            scratch=[
                pltpu.VMEM((TOK, 2 * WIDE), BF16),
                pltpu.VMEM((WIDE, HALF), BF16),
                pltpu.SemaphoreType.DMA((5,)),
            ],
        )
        return own, across(send), wide

    def finish(whole, count):
        (send,) = call(theirs_kernel, [((TOK, count * WIDE), F32)], whole)
        out = [((TOK, 2 * WIDE), BF16)] * count
        return call(finish_kernel, out, whole, across(send))

    own, got, wk = start(k, v, kmap, 60)
    send, k2, v2, kh, kl = call(
        keys_kernel, [((chips, rows + 8, LANES), F32), small, small, feats, feats], own, got, wk
    )
    first = exchange(send)
    own, got, wq = start(q, g, qmap, 32)
    q2, g2, qh, ql, numl, denl, sth, stl, cumk = call(
        queries_kernel,
        [small, small, feats, feats, flat, flat, scores, scores, feats32],
        own, got, wq, v2, kh, kl,
        flops=10**9,
    )
    send, den, dn, ksum = call(
        functools.partial(second_kernel, sizes),
        [((chips, 2 * rows, LANES), F32), flat, flat, sums],
        first, g2, qh, ql, denl,
    )
    second = exchange(send)
    gql, gkl, gvl = call(
        local_kernel, [feats32, feats32, flat], v2, qh, ql, kh, kl, sth, stl, dn, flops=10**9
    )
    send, dd = call(
        third_kernel,
        [((chips, rows + 8, LANES), F32), flat],
        second, g2, qh, ql, numl, den,
    )
    third = exchange(send)
    whole, gq_map, gkl = call(
        fourth_kernel,
        [flat, ((WIDE, LANES), F32), feats32],
        second, q2, wq, qh, ql, dn, dd, ksum, cumk, gql, gkl,
        flops=10**9,
    )
    (grad_q,) = finish(whole, 1)
    send, dz = call(
        functools.partial(fifth_kernel, sizes),
        [((chips, rows, LANES), F32), flat],
        third, k2, v2, kh, kl, gkl, gq_map,
    )
    got = exchange(send)
    (whole,) = call(
        sixth_kernel, [((BLOCK, 2 * WIDE), F32)], third, wk, kh, kl, gvl, dz, flops=10**9
    )
    grad_k, grad_v = finish(whole, 2)
    (send,) = call(sum_kernel, [((sizes["dp"], rows, LANES), F32)], got)
    got = lax.all_to_all(send, "dp", 0, 0)
    (send,) = call(sum_kernel, [((chips, rows, LANES), F32)], got)
    got = across(exchange(send))
    scale = float(BLOCK * chips * sizes["dp"]) ** (-0.5)
    heads = ((8, HALF, HALF), BF16)
    total_q, total_k = call(
        functools.partial(last_kernel, scale), [heads, heads], got.reshape(2 * WIDE, LANES)
    )
    shape = queries.shape
    return grad_q.reshape(shape), grad_k.reshape(shape), grad_v.reshape(shape), total_q, total_k


def physical(mesh):
    dp, ctx = mesh.devices.shape
    x = 4 if ctx % 8 == 0 and ctx > 8 else 2
    sizes = {"dp": dp, "z": ctx // (2 * x), "x": x, "core": 2}
    return Mesh(mesh.devices.reshape(tuple(sizes.values())), tuple(sizes)), sizes


def solution(mesh):
    inner, sizes = physical(mesh)
    tokens = P("dp", CTX, None)
    return jax.shard_map(
        functools.partial(per_device, sizes),
        mesh=inner,
        in_specs=(tokens,) * 4 + (P(), P()),
        out_specs=(tokens,) * 3 + (P(), P()),
        check_vma=False,
    )
```

```python
import functools

import jax
import jax.numpy as jnp
import numpy as np
from jax import lax
from jax.experimental import pallas as pl
from jax.experimental.pallas import tpu as pltpu
from jax.sharding import Mesh, PartitionSpec as P

F32 = jnp.float32
BF16 = jnp.bfloat16
CTX = ("z", "x", "core")
CHIPS = ("z", "x")
LANES = 128
HALF = 64
TOK = 128
BLOCK = 256
PAIRS = 2
WIDE = PAIRS * LANES


def nn(a, b):
    return lax.dot_general(a, b, (((1,), (0,)), ((), ())), preferred_element_type=F32)


def nt(a, b):
    return lax.dot_general(a, b, (((1,), (1,)), ((), ())), preferred_element_type=F32)


def split(x):
    hi = x.astype(BF16)
    return hi, (x - hi.astype(F32)).astype(BF16)


def both(op, a, w):
    rows = a[0].shape[0]
    out = op(jnp.concatenate(a, 0), w)
    return out[:rows] + out[rows:]


def three(op, a, b):
    return both(op, a, b[0]) + op(a[0], b[1])


def iota(shape, dim):
    return lax.broadcasted_iota(jnp.int32, shape, dim)


def low_lane(shape):
    return lax.rem(iota(shape, 1), LANES) < HALF


def diagonal(shape):
    return (lax.rem(iota(shape, 0), LANES) < HALF) == low_lane(shape)


def swap(x):
    return jnp.concatenate([x[HALF:], x[:HALF]], 0)


def pack(d):
    return jnp.where(diagonal((LANES, LANES)), d[:, :LANES], swap(d[:, LANES:]))


def unpack(x):
    diag = diagonal((LANES, LANES))
    return jnp.concatenate([jnp.where(diag, x, 0.0), jnp.where(diag, swap(x), 0.0)], 1)


def stacked(x):
    low = low_lane(x.shape)
    zero = jnp.zeros_like(x)
    return jnp.concatenate([jnp.where(low, x, zero), jnp.where(low, zero, x)], 0)


def side_by_side(x):
    return jnp.concatenate([x[:BLOCK], x[BLOCK:]], 1)


def block_ones():
    return jnp.where(diagonal((LANES, LANES)), 1.0, 0.0).astype(BF16)


def head_sum(x):
    return both(nn, split(x), block_ones())


def block_maps(maps_ref):
    twice = jnp.where(
        iota((HALF, LANES), 0) == lax.rem(iota((HALF, LANES), 1), HALF), 1.0, 0.0
    ).astype(BF16)
    wide = nn(maps_ref[...], twice)
    return jnp.where(diagonal(wide.shape), wide, 0.0).astype(BF16)


def cols(p, width=LANES):
    return slice(p * width, (p + 1) * width)


def softmaxes(z):
    low = low_lane(z.shape)
    inf = jnp.inf
    top = jnp.where(
        low,
        jnp.max(jnp.where(low, z, -inf), 1, keepdims=True),
        jnp.max(jnp.where(low, -inf, z), 1, keepdims=True),
    )
    bottom = jnp.where(
        low,
        jnp.min(jnp.where(low, z, inf), 1, keepdims=True),
        jnp.min(jnp.where(low, inf, z), 1, keepdims=True),
    )
    up = jnp.exp(z - top)
    down = jnp.exp(bottom - z)
    return up / head_sum(up), down / head_sum(down)


def core():
    return lax.axis_index("core")


def chip(sizes):
    return lax.axis_index("z") * sizes["x"] + lax.axis_index("x")


def causal(rows):
    return iota((rows, BLOCK), 1) <= lax.rem(iota((rows, BLOCK), 0), BLOCK)


def causal_back(rows):
    return iota((rows, BLOCK), 1) >= lax.rem(iota((rows, BLOCK), 0), BLOCK)


def start_kernel(a, b, maps, send, own, wide, other, few, sems):
    mine = pl.ds(pl.multiple_of(core() * WIDE, WIDE), WIDE)
    theirs = pl.ds(pl.multiple_of((1 - core()) * WIDE, WIDE), WIDE)
    copies = []
    for i, ref in enumerate((a, b)):
        here = pl.ds(i * WIDE, WIDE)
        copies.append(pltpu.make_async_copy(ref.at[:, theirs], other.at[:, here], sems.at[2 * i]))
        copies.append(pltpu.make_async_copy(ref.at[:, mine], own.at[:, here], sems.at[2 * i + 1]))
    copies.append(pltpu.make_async_copy(maps.at[mine, :], few, sems.at[4]))
    for copy in copies:
        copy.start()
    copies[4].wait()
    wide[...] = block_maps(few)
    for copy in copies[:4]:
        copy.wait()
    send[...] = other[...].astype(F32)


def assemble(own, got, first, second):
    here = pl.ds(pl.multiple_of(core() * TOK, TOK), TOK)
    there = pl.ds(pl.multiple_of((1 - core()) * TOK, TOK), TOK)
    for i, ref in enumerate((first, second)):
        lanes = slice(i * WIDE, (i + 1) * WIDE)
        ref[here, :] = own[:, lanes]
        ref[there, :] = got[1 - core(), :, lanes].astype(BF16)


def keys_kernel(own, got, wk, send, k, v, kh, kl):
    assemble(own, got, k, v)
    chips = send.shape[0]
    rows = WIDE // chips
    state, sums_p, sums_m = [], [], []
    for p in range(PAIRS):
        c = cols(p)
        pk, mk = softmaxes(nn(k[:, c], wk[c]))
        sums_p.append(jnp.sum(pk, 0, keepdims=True))
        sums_m.append(jnp.sum(mk, 0, keepdims=True))
        hi, lo = split(jnp.concatenate([pk, mk], 1))
        kh[:, cols(p, 2 * LANES)] = hi
        kl[:, cols(p, 2 * LANES)] = lo
        vt = v[:, c].T
        state.append(pack(nn(vt, hi) + nn(vt, lo)))
    send[:, :rows, :] = jnp.concatenate(state, 0).reshape(chips, rows, LANES)
    sums = jnp.concatenate(sums_p + sums_m + [jnp.zeros((4, LANES), F32)], 0)
    send[:, rows:, :] = jnp.broadcast_to(sums[None], (chips, 8, LANES))


def queries_kernel(own, got, wq, v, kh, kl, q, g, qh, ql, num, den):
    assemble(own, got, q, g)
    mask = causal(2 * BLOCK)
    for p in range(PAIRS):
        c = cols(p)
        w = cols(p, 2 * LANES)
        pq, mq = softmaxes(nn(q[:, c], wq[c]))
        q2 = split(jnp.concatenate([pq, mq], 1))
        qh[:, w], ql[:, w] = q2
        k2 = (kh[:, w], kl[:, w])
        scores = three(nt, (stacked(q2[0]), stacked(q2[1])), k2)
        scores = side_by_side(jnp.where(mask, scores, 0.0))
        v2 = stacked(v[:, c])
        ones = stacked(jnp.ones((BLOCK, LANES), BF16))
        out = both(nn, split(scores), jnp.concatenate([v2, ones], 1))
        num[:, c] = out[:, :LANES]
        den[:, c] = out[:, LANES:]


def second_kernel(sizes, got, g, qh, ql, denl, send, den, dn, ksum):
    chips = send.shape[0]
    rows = WIDE // chips
    me = chip(sizes)
    acc = jnp.zeros((8, LANES), F32)
    run = jnp.zeros((rows, LANES), F32)
    for m in range(chips):
        send[m, :rows, :] = run
        run = run + got[m, :rows, :]
        acc = acc + jnp.where(m < me, got[m, rows:, :], 0.0)
    ksum[...] = acc
    diag = diagonal((LANES, 2 * LANES))
    out = []
    for p in range(PAIRS):
        c = cols(p)
        w = cols(p, 2 * LANES)
        q2 = (qh[:, w], ql[:, w])
        sums = jnp.concatenate([acc[p : p + 1], acc[p + PAIRS : p + PAIRS + 1]], 1)
        sums = jnp.where(diag, jnp.broadcast_to(sums, (LANES, 2 * LANES)), 0.0)
        d = denl[:, c] + three(nt, q2, split(sums))
        den[:, c] = d
        scaled = g[:, c].astype(F32) / d
        dn[:, c] = scaled
        out.append(pack(three(nn, split(scaled.T), q2)))
    send[:, rows:, :] = jnp.concatenate(out, 0).reshape(chips, rows, LANES)


def local_kernel(v, qh, ql, kh, kl, dn, gql, gvl, token):
    token[...] = jnp.zeros_like(token)
    mask = causal(2 * BLOCK)
    back_mask = causal_back(2 * BLOCK)
    for p in range(PAIRS):
        c = cols(p)
        w = cols(p, 2 * LANES)
        q2 = (qh[:, w], ql[:, w])
        k2 = (kh[:, w], kl[:, w])
        v2 = v[:, c]
        s2 = split(dn[:, c])
        d2 = (stacked(s2[0]), stacked(s2[1]))
        mixing = split(side_by_side(jnp.where(mask, both(nt, d2, v2), 0.0)))
        gql[:, w] = three(nn, mixing, (stacked(k2[0]), stacked(k2[1])))
        scores = three(nt, (stacked(k2[0]), stacked(k2[1])), q2)
        scores = split(side_by_side(jnp.where(back_mask, scores, 0.0)))
        gvl[:, c] = three(nn, scores, d2)


def third_kernel(got, g, qh, ql, numl, den, _, send, dd):
    chips = send.shape[0]
    rows = WIDE // chips
    run = jnp.zeros((rows, LANES), F32)
    for m in reversed(range(chips)):
        send[m, :rows, :] = run
        run = run + got[m, rows:, :]
    state = got[:, :rows, :].reshape(WIDE, LANES)
    sums_p, sums_m = [], []
    for p in range(PAIRS):
        c = cols(p)
        w = cols(p, 2 * LANES)
        q2 = (qh[:, w], ql[:, w])
        numer = numl[:, c] + three(nt, q2, split(unpack(state[c])))
        d = den[:, c]
        dden = -head_sum(g[:, c].astype(F32) * (numer / d)) / d
        dd[:, c] = dden
        full = q2[0].astype(F32) + q2[1].astype(F32)
        sums_p.append(jnp.sum(full[:, :LANES] * dden, 0, keepdims=True))
        sums_m.append(jnp.sum(full[:, LANES:] * dden, 0, keepdims=True))
    sums = jnp.concatenate(sums_p + sums_m + [jnp.zeros((4, LANES), F32)], 0)
    send[:, rows:, :] = jnp.broadcast_to(sums[None], (chips, 8, LANES))


def feature_back(f2, grad):
    full = f2[0].astype(F32) + f2[1].astype(F32)
    plus, minus = full[:, :LANES], full[:, LANES:]
    first, second = grad[:, :LANES], grad[:, LANES:]
    return plus * (first - head_sum(plus * first)) - minus * (second - head_sum(minus * second))


def twice(x):
    return jnp.concatenate([x, x], 1)


def fourth_kernel(got, q, v, wq, qh, ql, kh, kl, dn, dd, ksum, gql, whole, gq_map, gk_all):
    rows = WIDE // got.shape[0]
    state = got[:, :rows, :].reshape(WIDE, LANES)
    tri = jnp.where(causal(BLOCK), 1.0, 0.0).astype(BF16)
    tri_back = jnp.where(causal_back(BLOCK), 1.0, 0.0).astype(BF16)
    back_mask = causal_back(2 * BLOCK)
    for p in range(PAIRS):
        c = cols(p)
        w = cols(p, 2 * LANES)
        q2 = (qh[:, w], ql[:, w])
        dden = twice(dd[:, c])
        sums = jnp.concatenate([ksum[p : p + 1, :], ksum[p + PAIRS : p + PAIRS + 1, :]], 1)
        s2 = split(dn[:, c])
        grad = gql[:, w] + three(nn, s2, split(unpack(state[c])))
        grad = grad + dden * (sums + (nn(tri, kh[:, w]) + nn(tri, kl[:, w])))
        dzq = feature_back(q2, grad)
        z2 = split(dzq)
        whole[:, c] = both(nt, z2, wq[c])
        qt = q[:, c].T
        gq_map[c, :] = nn(qt, z2[0]) + nn(qt, z2[1])
        later = split((q2[0].astype(F32) + q2[1].astype(F32)) * dden)
        vv = stacked(v[:, c])
        back = jnp.where(back_mask, nt(vv, s2[0]) + nt(vv, s2[1]), 0.0)
        back = split(side_by_side(back))
        gk = three(nn, back, (stacked(q2[0]), stacked(q2[1])))
        gk_all[:, w] = gk + (nn(tri_back, later[0]) + nn(tri_back, later[1]))


def fifth_kernel(sizes, got, k, v, kh, kl, gkl, gq_map, _, send, dz):
    chips = send.shape[0]
    rows = WIDE // chips
    me = chip(sizes)
    acc = jnp.zeros((8, LANES), F32)
    for m in range(chips):
        acc = acc + jnp.where(m > me, got[m, rows:, :], 0.0)
    later = got[:, :rows, :].reshape(WIDE, LANES)
    out = []
    for p in range(PAIRS):
        c = cols(p)
        w = cols(p, 2 * LANES)
        k2 = (kh[:, w], kl[:, w])
        sums = jnp.concatenate([acc[p : p + 1], acc[p + PAIRS : p + PAIRS + 1]], 1)
        grad = gkl[:, w] + sums + nn(
            twice(v[:, c]), jnp.concatenate(split(unpack(later[c])), 0)
        )
        dzk = feature_back(k2, grad)
        dz[:, c] = dzk
        z2 = split(dzk)
        kt = k[:, c].T
        out.append(
            pack(jnp.concatenate([gq_map[c, :], nn(kt, z2[0]) + nn(kt, z2[1])], 1))
        )
    send[...] = jnp.concatenate(out, 0).reshape(chips, rows, LANES)


def sixth_kernel(got, wk, kh, kl, gvl, dz, _, whole):
    rows = WIDE // got.shape[0]
    later = got[:, :rows, :].reshape(WIDE, LANES)
    for p in range(PAIRS):
        c = cols(p)
        w = cols(p, 2 * LANES)
        whole[:, c] = both(nt, split(dz[:, c]), wk[c])
        grad = gvl[:, c] + three(nt, (kh[:, w], kl[:, w]), split(unpack(later[c])))
        whole[:, WIDE + p * LANES : WIDE + (p + 1) * LANES] = grad


def theirs_kernel(whole, send):
    send[...] = whole[pl.ds(pl.multiple_of((1 - core()) * TOK, TOK), TOK), :]


def finish_kernel(whole, got, *outs):
    *outs, token = outs
    token[...] = jnp.zeros_like(token)
    own = whole[pl.ds(pl.multiple_of(core() * TOK, TOK), TOK), :]
    other = got[1 - core()]
    first = core() == 0
    for i, out in enumerate(outs):
        lanes = slice(i * WIDE, (i + 1) * WIDE)
        a, b = own[:, lanes], other[:, lanes]
        out[:, :WIDE] = jnp.where(first, a, b).astype(BF16)
        out[:, WIDE:] = jnp.where(first, b, a).astype(BF16)


def sum_kernel(got, *rest):
    send = rest[-1]
    total = got[0]
    for m in range(1, got.shape[0]):
        total = total + got[m]
    send[...] = jnp.broadcast_to(total[None], send.shape)


def last_kernel(scale, got, gq, gk):
    for p in range(2 * PAIRS):
        x = got[cols(p), :] * scale
        y = pltpu.roll(x, HALF, 1)
        gq[2 * p] = x[:HALF, :HALF].astype(BF16)
        gq[2 * p + 1] = y[HALF:, :HALF].astype(BF16)
        gk[2 * p] = x[HALF:, :HALF].astype(BF16)
        gk[2 * p + 1] = y[:HALF, :HALF].astype(BF16)


def call(kernel, outs, *args, flops=10**8, space=pltpu.VMEM, scratch=(), room=32):
    shapes = [jax.ShapeDtypeStruct(shape, dtype) for shape, dtype in outs]
    moved = sum(a.size * a.dtype.itemsize for a in (*args, *shapes))
    return pl.pallas_call(
        kernel,
        out_shape=shapes,
        in_specs=[pl.BlockSpec(memory_space=space)] * len(args),
        out_specs=[pl.BlockSpec(memory_space=pltpu.VMEM)] * len(outs),
        scratch_shapes=scratch,
        compiler_params=pltpu.CompilerParams(vmem_limit_bytes=int(room * 2**20)),
        cost_estimate=pl.CostEstimate(flops=flops, bytes_accessed=moved, transcendentals=0),
    )(*args)


def per_device(sizes, queries, keys, values, upstream, query_map, key_map):
    chips = sizes["z"] * sizes["x"]
    rows = WIDE // chips
    q, k, v, g = (a.reshape(TOK, 2 * WIDE) for a in (queries, keys, values, upstream))
    qmap = query_map.reshape(2 * WIDE, HALF)
    kmap = key_map.reshape(2 * WIDE, HALF)
    feats = ((BLOCK, 2 * WIDE), BF16)
    feats32 = ((BLOCK, 2 * WIDE), F32)
    flat = ((BLOCK, WIDE), F32)
    small = ((BLOCK, WIDE), BF16)
    sums = ((8, LANES), F32)

    def across(a):
        return lax.all_gather(a, "core")

    def exchange(a):
        return lax.all_to_all(a, CHIPS, 0, 0)

    def start(a, b, maps, room):
        send, own, wide = call(
            start_kernel,
            [((TOK, 2 * WIDE), F32), ((TOK, 2 * WIDE), BF16), ((WIDE, LANES), BF16)],
            a, b, maps,
            space=pl.ANY,
            room=room,
            scratch=[
                pltpu.VMEM((TOK, 2 * WIDE), BF16),
                pltpu.VMEM((WIDE, HALF), BF16),
                pltpu.SemaphoreType.DMA((5,)),
            ],
        )
        return own, across(send), wide

    def finish(whole, count):
        (send,) = call(theirs_kernel, [((TOK, count * WIDE), F32)], whole)
        out = [((TOK, 2 * WIDE), BF16)] * count + [sums]
        return call(finish_kernel, out, whole, across(send))

    own, got, wk = start(k, v, kmap, 60)
    send, k2, v2, kh, kl = call(
        keys_kernel, [((chips, rows + 8, LANES), F32), small, small, feats, feats], own, got, wk
    )
    first = exchange(send)
    own, got, wq = start(q, g, qmap, 32)
    q2, g2, qh, ql, numl, denl = call(
        queries_kernel,
        [small, small, feats, feats, flat, flat],
        own, got, wq, v2, kh, kl,
        flops=10**9,
    )
    send, den, dn, ksum = call(
        functools.partial(second_kernel, sizes),
        [((chips, 2 * rows, LANES), F32), flat, flat, sums],
        first, g2, qh, ql, denl,
    )
    second = exchange(send)
    gql, gvl, token = call(
        local_kernel, [feats32, flat, sums], v2, qh, ql, kh, kl, dn, flops=10**9
    )
    send, dd = call(
        third_kernel,
        [((chips, rows + 8, LANES), F32), flat],
        second, g2, qh, ql, numl, den, token,
    )
    third = exchange(send)
    whole, gq_map, gkl = call(
        fourth_kernel,
        [flat, ((WIDE, LANES), F32), feats32],
        second, q2, v2, wq, qh, ql, kh, kl, dn, dd, ksum, gql,
        flops=10**9,
    )
    grad_q, token = finish(whole, 1)
    send, dz = call(
        functools.partial(fifth_kernel, sizes),
        [((chips, rows, LANES), F32), flat],
        third, k2, v2, kh, kl, gkl, gq_map, token,
    )
    got = exchange(send)
    (send,) = call(sum_kernel, [((sizes["dp"], rows, LANES), F32)], got)
    (whole,) = call(
        sixth_kernel,
        [((BLOCK, 2 * WIDE), F32)],
        third, wk, kh, kl, gvl, dz, send,
        flops=10**9,
    )
    grad_k, grad_v, token = finish(whole, 2)
    got = lax.all_to_all(send, "dp", 0, 0)
    (send,) = call(sum_kernel, [((chips, rows, LANES), F32)], got, token)
    got = across(exchange(send))
    scale = float(BLOCK * chips * sizes["dp"]) ** (-0.5)
    heads = ((8, HALF, HALF), BF16)
    total_q, total_k = call(
        functools.partial(last_kernel, scale), [heads, heads], got.reshape(2 * WIDE, LANES)
    )
    shape = queries.shape
    return grad_q.reshape(shape), grad_k.reshape(shape), grad_v.reshape(shape), total_q, total_k


def physical(mesh):
    dp, ctx = mesh.devices.shape
    x = 4 if ctx % 8 == 0 and ctx > 8 else 2
    sizes = {"dp": dp, "z": ctx // (2 * x), "x": x, "core": 2}
    return Mesh(mesh.devices.reshape(tuple(sizes.values())), tuple(sizes)), sizes


def solution(mesh):
    inner, sizes = physical(mesh)
    tokens = P("dp", CTX, None)
    return jax.shard_map(
        functools.partial(per_device, sizes),
        mesh=inner,
        in_specs=(tokens,) * 4 + (P(), P()),
        out_specs=(tokens,) * 3 + (P(), P()),
        check_vma=False,
    )
```

```python
import functools

import jax
import jax.numpy as jnp
import numpy as np
from jax import lax
from jax.experimental import pallas as pl
from jax.experimental.pallas import tpu as pltpu
from jax.sharding import Mesh, PartitionSpec as P

F32 = jnp.float32
BF16 = jnp.bfloat16
CTX = ("z", "x", "core")
CHIPS = ("z", "x")
LANES = 128
HALF = 64
TOK = 128
BLOCK = 256
PAIRS = 2
WIDE = PAIRS * LANES


def nn(a, b):
    return lax.dot_general(a, b, (((1,), (0,)), ((), ())), preferred_element_type=F32)


def nt(a, b):
    return lax.dot_general(a, b, (((1,), (1,)), ((), ())), preferred_element_type=F32)


def split(x):
    hi = x.astype(BF16)
    return hi, (x - hi.astype(F32)).astype(BF16)


def both(op, a, w):
    rows = a[0].shape[0]
    out = op(jnp.concatenate(a, 0), w)
    return out[:rows] + out[rows:]


def three(op, a, b):
    return both(op, a, b[0]) + op(a[0], b[1])


def iota(shape, dim):
    return lax.broadcasted_iota(jnp.int32, shape, dim)


def low_lane(shape):
    return lax.rem(iota(shape, 1), LANES) < HALF


def diagonal(shape):
    return (lax.rem(iota(shape, 0), LANES) < HALF) == low_lane(shape)


def swap(x):
    return jnp.concatenate([x[HALF:], x[:HALF]], 0)


def pack(d):
    return jnp.where(diagonal((LANES, LANES)), d[:, :LANES], swap(d[:, LANES:]))


def unpack(x):
    diag = diagonal((LANES, LANES))
    return jnp.concatenate([jnp.where(diag, x, 0.0), jnp.where(diag, swap(x), 0.0)], 1)


def stacked(x):
    low = low_lane(x.shape)
    zero = jnp.zeros_like(x)
    return jnp.concatenate([jnp.where(low, x, zero), jnp.where(low, zero, x)], 0)


def side_by_side(x):
    return jnp.concatenate([x[:BLOCK], x[BLOCK:]], 1)


def block_ones():
    return jnp.where(diagonal((LANES, LANES)), 1.0, 0.0).astype(BF16)


def head_sum(x):
    return both(nn, split(x), block_ones())


def block_maps(maps_ref):
    twice = jnp.where(
        iota((HALF, LANES), 0) == lax.rem(iota((HALF, LANES), 1), HALF), 1.0, 0.0
    ).astype(BF16)
    wide = nn(maps_ref[...], twice)
    return jnp.where(diagonal(wide.shape), wide, 0.0).astype(BF16)


def cols(p, width=LANES):
    return slice(p * width, (p + 1) * width)


def softmaxes(z):
    low = low_lane(z.shape)
    inf = jnp.inf
    top = jnp.where(
        low,
        jnp.max(jnp.where(low, z, -inf), 1, keepdims=True),
        jnp.max(jnp.where(low, -inf, z), 1, keepdims=True),
    )
    bottom = jnp.where(
        low,
        jnp.min(jnp.where(low, z, inf), 1, keepdims=True),
        jnp.min(jnp.where(low, inf, z), 1, keepdims=True),
    )
    up = jnp.exp(z - top)
    down = jnp.exp(bottom - z)
    return up / head_sum(up), down / head_sum(down)


def core():
    return lax.axis_index("core")


def chip(sizes):
    return lax.axis_index("z") * sizes["x"] + lax.axis_index("x")


def causal(rows):
    return iota((rows, BLOCK), 1) <= lax.rem(iota((rows, BLOCK), 0), BLOCK)


def causal_back(rows):
    return iota((rows, BLOCK), 1) >= lax.rem(iota((rows, BLOCK), 0), BLOCK)


def start_kernel(a, b, maps, send, own, wide, other, few, sems):
    mine = pl.ds(pl.multiple_of(core() * WIDE, WIDE), WIDE)
    theirs = pl.ds(pl.multiple_of((1 - core()) * WIDE, WIDE), WIDE)
    copies = []
    for i, ref in enumerate((a, b)):
        here = pl.ds(i * WIDE, WIDE)
        copies.append(pltpu.make_async_copy(ref.at[:, theirs], other.at[:, here], sems.at[2 * i]))
        copies.append(pltpu.make_async_copy(ref.at[:, mine], own.at[:, here], sems.at[2 * i + 1]))
    copies.append(pltpu.make_async_copy(maps.at[mine, :], few, sems.at[4]))
    for copy in copies:
        copy.start()
    copies[4].wait()
    wide[...] = block_maps(few)
    for copy in copies[:4]:
        copy.wait()
    send[...] = other[...].astype(F32)


def assemble(own, got, first, second):
    here = pl.ds(pl.multiple_of(core() * TOK, TOK), TOK)
    there = pl.ds(pl.multiple_of((1 - core()) * TOK, TOK), TOK)
    for i, ref in enumerate((first, second)):
        lanes = slice(i * WIDE, (i + 1) * WIDE)
        ref[here, :] = own[:, lanes]
        ref[there, :] = got[1 - core(), :, lanes].astype(BF16)


def keys_kernel(own, got, wk, send, k, v, kh, kl):
    assemble(own, got, k, v)
    chips = send.shape[0]
    rows = WIDE // chips
    state, sums_p, sums_m = [], [], []
    for p in range(PAIRS):
        c = cols(p)
        pk, mk = softmaxes(nn(k[:, c], wk[c]))
        sums_p.append(jnp.sum(pk, 0, keepdims=True))
        sums_m.append(jnp.sum(mk, 0, keepdims=True))
        hi, lo = split(jnp.concatenate([pk, mk], 1))
        kh[:, cols(p, 2 * LANES)] = hi
        kl[:, cols(p, 2 * LANES)] = lo
        vt = v[:, c].T
        state.append(pack(nn(vt, hi) + nn(vt, lo)))
    send[:, :rows, :] = jnp.concatenate(state, 0).reshape(chips, rows, LANES)
    sums = jnp.concatenate(sums_p + sums_m + [jnp.zeros((4, LANES), F32)], 0)
    send[:, rows:, :] = jnp.broadcast_to(sums[None], (chips, 8, LANES))


def queries_kernel(own, got, wq, v, kh, kl, q, g, qh, ql, num, den):
    assemble(own, got, q, g)
    mask = causal(2 * BLOCK)
    for p in range(PAIRS):
        c = cols(p)
        w = cols(p, 2 * LANES)
        pq, mq = softmaxes(nn(q[:, c], wq[c]))
        q2 = split(jnp.concatenate([pq, mq], 1))
        qh[:, w], ql[:, w] = q2
        k2 = (kh[:, w], kl[:, w])
        scores = three(nt, (stacked(q2[0]), stacked(q2[1])), k2)
        scores = side_by_side(jnp.where(mask, scores, 0.0))
        v2 = stacked(v[:, c])
        ones = stacked(jnp.ones((BLOCK, LANES), BF16))
        out = both(nn, split(scores), jnp.concatenate([v2, ones], 1))
        num[:, c] = out[:, :LANES]
        den[:, c] = out[:, LANES:]


def second_kernel(sizes, got, g, qh, ql, denl, send, den, dn, ksum):
    chips = send.shape[0]
    rows = WIDE // chips
    me = chip(sizes)
    acc = jnp.zeros((8, LANES), F32)
    run = jnp.zeros((rows, LANES), F32)
    for m in range(chips):
        send[m, :rows, :] = run
        run = run + got[m, :rows, :]
        acc = acc + jnp.where(m < me, got[m, rows:, :], 0.0)
    ksum[...] = acc
    diag = diagonal((LANES, 2 * LANES))
    out = []
    for p in range(PAIRS):
        c = cols(p)
        w = cols(p, 2 * LANES)
        q2 = (qh[:, w], ql[:, w])
        sums = jnp.concatenate([acc[p : p + 1], acc[p + PAIRS : p + PAIRS + 1]], 1)
        sums = jnp.where(diag, jnp.broadcast_to(sums, (LANES, 2 * LANES)), 0.0)
        d = denl[:, c] + three(nt, q2, split(sums))
        den[:, c] = d
        scaled = g[:, c].astype(F32) / d
        dn[:, c] = scaled
        out.append(pack(three(nn, split(scaled.T), q2)))
    send[:, rows:, :] = jnp.concatenate(out, 0).reshape(chips, rows, LANES)


def local_kernel(v, qh, ql, kh, kl, dn, gql, gvl, token):
    token[...] = jnp.zeros_like(token)
    mask = causal(2 * BLOCK)
    back_mask = causal_back(2 * BLOCK)
    for p in range(PAIRS):
        c = cols(p)
        w = cols(p, 2 * LANES)
        q2 = (qh[:, w], ql[:, w])
        k2 = (kh[:, w], kl[:, w])
        v2 = v[:, c]
        s2 = split(dn[:, c])
        d2 = (stacked(s2[0]), stacked(s2[1]))
        mixing = split(side_by_side(jnp.where(mask, both(nt, d2, v2), 0.0)))
        gql[:, w] = three(nn, mixing, (stacked(k2[0]), stacked(k2[1])))
        scores = three(nt, (stacked(k2[0]), stacked(k2[1])), q2)
        scores = split(side_by_side(jnp.where(back_mask, scores, 0.0)))
        gvl[:, c] = three(nn, scores, d2)


def third_kernel(got, g, qh, ql, numl, den, _, send, dd):
    chips = send.shape[0]
    rows = WIDE // chips
    run = jnp.zeros((rows, LANES), F32)
    for m in reversed(range(chips)):
        send[m, :rows, :] = run
        run = run + got[m, rows:, :]
    state = got[:, :rows, :].reshape(WIDE, LANES)
    sums_p, sums_m = [], []
    for p in range(PAIRS):
        c = cols(p)
        w = cols(p, 2 * LANES)
        q2 = (qh[:, w], ql[:, w])
        numer = numl[:, c] + three(nt, q2, split(unpack(state[c])))
        d = den[:, c]
        dden = -head_sum(g[:, c].astype(F32) * (numer / d)) / d
        dd[:, c] = dden
        full = q2[0].astype(F32) + q2[1].astype(F32)
        sums_p.append(jnp.sum(full[:, :LANES] * dden, 0, keepdims=True))
        sums_m.append(jnp.sum(full[:, LANES:] * dden, 0, keepdims=True))
    sums = jnp.concatenate(sums_p + sums_m + [jnp.zeros((4, LANES), F32)], 0)
    send[:, rows:, :] = jnp.broadcast_to(sums[None], (chips, 8, LANES))


def feature_back(f2, grad):
    full = f2[0].astype(F32) + f2[1].astype(F32)
    plus, minus = full[:, :LANES], full[:, LANES:]
    first, second = grad[:, :LANES], grad[:, LANES:]
    return plus * (first - head_sum(plus * first)) - minus * (second - head_sum(minus * second))


def twice(x):
    return jnp.concatenate([x, x], 1)


def fourth_kernel(got, q, v, wq, qh, ql, kh, kl, dn, dd, ksum, gql, whole, gq_map, gk_all):
    rows = WIDE // got.shape[0]
    state = got[:, :rows, :].reshape(WIDE, LANES)
    tri = jnp.where(causal(BLOCK), 1.0, 0.0).astype(BF16)
    tri_back = jnp.where(causal_back(BLOCK), 1.0, 0.0).astype(BF16)
    back_mask = causal_back(2 * BLOCK)
    for p in range(PAIRS):
        c = cols(p)
        w = cols(p, 2 * LANES)
        q2 = (qh[:, w], ql[:, w])
        dden = twice(dd[:, c])
        sums = jnp.concatenate([ksum[p : p + 1, :], ksum[p + PAIRS : p + PAIRS + 1, :]], 1)
        s2 = split(dn[:, c])
        grad = gql[:, w] + three(nn, s2, split(unpack(state[c])))
        grad = grad + dden * (sums + (nn(tri, kh[:, w]) + nn(tri, kl[:, w])))
        dzq = feature_back(q2, grad)
        z2 = split(dzq)
        whole[:, c] = both(nt, z2, wq[c])
        qt = q[:, c].T
        gq_map[c, :] = nn(qt, z2[0]) + nn(qt, z2[1])
        later = split((q2[0].astype(F32) + q2[1].astype(F32)) * dden)
        vv = stacked(v[:, c])
        back = jnp.where(back_mask, nt(vv, s2[0]) + nt(vv, s2[1]), 0.0)
        back = split(side_by_side(back))
        gk = three(nn, back, (stacked(q2[0]), stacked(q2[1])))
        gk_all[:, w] = gk + (nn(tri_back, later[0]) + nn(tri_back, later[1]))


def fifth_kernel(sizes, got, k, v, kh, kl, gkl, gq_map, _, send, dz):
    chips = send.shape[0]
    rows = WIDE // chips
    me = chip(sizes)
    acc = jnp.zeros((8, LANES), F32)
    for m in range(chips):
        acc = acc + jnp.where(m > me, got[m, rows:, :], 0.0)
    later = got[:, :rows, :].reshape(WIDE, LANES)
    out = []
    for p in range(PAIRS):
        c = cols(p)
        w = cols(p, 2 * LANES)
        k2 = (kh[:, w], kl[:, w])
        sums = jnp.concatenate([acc[p : p + 1], acc[p + PAIRS : p + PAIRS + 1]], 1)
        grad = gkl[:, w] + sums + nn(
            twice(v[:, c]), jnp.concatenate(split(unpack(later[c])), 0)
        )
        dzk = feature_back(k2, grad)
        dz[:, c] = dzk
        z2 = split(dzk)
        kt = k[:, c].T
        out.append(
            pack(jnp.concatenate([gq_map[c, :], nn(kt, z2[0]) + nn(kt, z2[1])], 1))
        )
    send[...] = jnp.concatenate(out, 0).reshape(chips, rows, LANES)


def sixth_kernel(got, wk, kh, kl, gvl, dz, whole):
    rows = WIDE // got.shape[0]
    later = got[:, :rows, :].reshape(WIDE, LANES)
    for p in range(PAIRS):
        c = cols(p)
        w = cols(p, 2 * LANES)
        whole[:, c] = both(nt, split(dz[:, c]), wk[c])
        grad = gvl[:, c] + three(nt, (kh[:, w], kl[:, w]), split(unpack(later[c])))
        whole[:, WIDE + p * LANES : WIDE + (p + 1) * LANES] = grad


def theirs_kernel(whole, send):
    send[...] = whole[pl.ds(pl.multiple_of((1 - core()) * TOK, TOK), TOK), :]


def finish_kernel(whole, got, *outs):
    *outs, token = outs
    token[...] = jnp.zeros_like(token)
    own = whole[pl.ds(pl.multiple_of(core() * TOK, TOK), TOK), :]
    other = got[1 - core()]
    first = core() == 0
    for i, out in enumerate(outs):
        lanes = slice(i * WIDE, (i + 1) * WIDE)
        a, b = own[:, lanes], other[:, lanes]
        out[:, :WIDE] = jnp.where(first, a, b).astype(BF16)
        out[:, WIDE:] = jnp.where(first, b, a).astype(BF16)


def sum_kernel(got, *rest):
    send = rest[-1]
    total = got[0]
    for m in range(1, got.shape[0]):
        total = total + got[m]
    send[...] = jnp.broadcast_to(total[None], send.shape)


def sum_cores_kernel(got, send):
    acc = [got[0], got[1]]
    for m in range(2, got.shape[0]):
        acc[m % 2] = acc[m % 2] + got[m]
    send[...] = jnp.broadcast_to(jnp.concatenate(acc, 0)[None], send.shape)


def last_kernel(scale, got, gq, gk):
    rows = got.shape[1] // 2
    cores = [got[:, :rows, :].reshape(WIDE, LANES), got[:, rows:, :].reshape(WIDE, LANES)]
    for p in range(2 * PAIRS):
        x = cores[p // PAIRS][cols(p % PAIRS), :] * scale
        y = pltpu.roll(x, HALF, 1)
        gq[2 * p] = x[:HALF, :HALF].astype(BF16)
        gq[2 * p + 1] = y[HALF:, :HALF].astype(BF16)
        gk[2 * p] = x[HALF:, :HALF].astype(BF16)
        gk[2 * p + 1] = y[:HALF, :HALF].astype(BF16)


def call(kernel, outs, *args, flops=10**8, space=pltpu.VMEM, scratch=(), room=32):
    shapes = [jax.ShapeDtypeStruct(shape, dtype) for shape, dtype in outs]
    moved = sum(a.size * a.dtype.itemsize for a in (*args, *shapes))
    return pl.pallas_call(
        kernel,
        out_shape=shapes,
        in_specs=[pl.BlockSpec(memory_space=space)] * len(args),
        out_specs=[pl.BlockSpec(memory_space=pltpu.VMEM)] * len(outs),
        scratch_shapes=scratch,
        compiler_params=pltpu.CompilerParams(vmem_limit_bytes=int(room * 2**20)),
        cost_estimate=pl.CostEstimate(flops=flops, bytes_accessed=moved, transcendentals=0),
    )(*args)


def per_device(sizes, queries, keys, values, upstream, query_map, key_map):
    chips = sizes["z"] * sizes["x"]
    rows = WIDE // chips
    q, k, v, g = (a.reshape(TOK, 2 * WIDE) for a in (queries, keys, values, upstream))
    qmap = query_map.reshape(2 * WIDE, HALF)
    kmap = key_map.reshape(2 * WIDE, HALF)
    feats = ((BLOCK, 2 * WIDE), BF16)
    feats32 = ((BLOCK, 2 * WIDE), F32)
    flat = ((BLOCK, WIDE), F32)
    small = ((BLOCK, WIDE), BF16)
    sums = ((8, LANES), F32)

    def across(a):
        return lax.all_gather(a, "core")

    def exchange(a):
        return lax.all_to_all(a, CHIPS, 0, 0)

    def start(a, b, maps, room):
        send, own, wide = call(
            start_kernel,
            [((TOK, 2 * WIDE), F32), ((TOK, 2 * WIDE), BF16), ((WIDE, LANES), BF16)],
            a, b, maps,
            space=pl.ANY,
            room=room,
            scratch=[
                pltpu.VMEM((TOK, 2 * WIDE), BF16),
                pltpu.VMEM((WIDE, HALF), BF16),
                pltpu.SemaphoreType.DMA((5,)),
            ],
        )
        return own, across(send), wide

    def finish(whole, count):
        (send,) = call(theirs_kernel, [((TOK, count * WIDE), F32)], whole)
        out = [((TOK, 2 * WIDE), BF16)] * count + [sums]
        return call(finish_kernel, out, whole, across(send))

    own, got, wk = start(k, v, kmap, 60)
    send, k2, v2, kh, kl = call(
        keys_kernel, [((chips, rows + 8, LANES), F32), small, small, feats, feats], own, got, wk
    )
    first = exchange(send)
    own, got, wq = start(q, g, qmap, 32)
    q2, g2, qh, ql, numl, denl = call(
        queries_kernel,
        [small, small, feats, feats, flat, flat],
        own, got, wq, v2, kh, kl,
        flops=10**9,
    )
    send, den, dn, ksum = call(
        functools.partial(second_kernel, sizes),
        [((chips, 2 * rows, LANES), F32), flat, flat, sums],
        first, g2, qh, ql, denl,
    )
    second = exchange(send)
    gql, gvl, token = call(
        local_kernel, [feats32, flat, sums], v2, qh, ql, kh, kl, dn, flops=10**9
    )
    send, dd = call(
        third_kernel,
        [((chips, rows + 8, LANES), F32), flat],
        second, g2, qh, ql, numl, den, token,
    )
    third = exchange(send)
    whole, gq_map, gkl = call(
        fourth_kernel,
        [flat, ((WIDE, LANES), F32), feats32],
        second, q2, v2, wq, qh, ql, kh, kl, dn, dd, ksum, gql,
        flops=10**9,
    )
    grad_q, token = finish(whole, 1)
    send, dz = call(
        functools.partial(fifth_kernel, sizes),
        [((chips, rows, LANES), F32), flat],
        third, k2, v2, kh, kl, gkl, gq_map, token,
    )
    got = exchange(send)
    (whole,) = call(
        sixth_kernel, [((BLOCK, 2 * WIDE), F32)], third, wk, kh, kl, gvl, dz, flops=10**9
    )
    grad_k, grad_v, token = finish(whole, 2)
    others = sizes["dp"] * sizes["core"]
    (send,) = call(sum_kernel, [((others, rows, LANES), F32)], got, token)
    got = lax.all_to_all(send, ("dp", "core"), 0, 0)
    (send,) = call(sum_cores_kernel, [((chips, 2 * rows, LANES), F32)], got)
    got = exchange(send)
    scale = float(BLOCK * chips * sizes["dp"]) ** (-0.5)
    heads = ((8, HALF, HALF), BF16)
    total_q, total_k = call(
        functools.partial(last_kernel, scale), [heads, heads], got
    )
    shape = queries.shape
    return grad_q.reshape(shape), grad_k.reshape(shape), grad_v.reshape(shape), total_q, total_k


def physical(mesh):
    dp, ctx = mesh.devices.shape
    x = 4 if ctx % 8 == 0 and ctx > 8 else 2
    sizes = {"dp": dp, "z": ctx // (2 * x), "x": x, "core": 2}
    return Mesh(mesh.devices.reshape(tuple(sizes.values())), tuple(sizes)), sizes


def solution(mesh):
    inner, sizes = physical(mesh)
    tokens = P("dp", CTX, None)
    return jax.shard_map(
        functools.partial(per_device, sizes),
        mesh=inner,
        in_specs=(tokens,) * 4 + (P(), P()),
        out_specs=(tokens,) * 3 + (P(), P()),
        check_vma=False,
    )
```

```python
import functools

import jax
import jax.numpy as jnp
import numpy as np
from jax import lax
from jax.experimental import pallas as pl
from jax.experimental.pallas import tpu as pltpu
from jax.sharding import Mesh, PartitionSpec as P

F32 = jnp.float32
BF16 = jnp.bfloat16
CTX = ("z", "x", "core")
CHIPS = ("z", "x")
LANES = 128
HALF = 64
TOK = 128
BLOCK = 256
PAIRS = 2
WIDE = PAIRS * LANES


def nn(a, b):
    return lax.dot_general(a, b, (((1,), (0,)), ((), ())), preferred_element_type=F32)


def nt(a, b):
    return lax.dot_general(a, b, (((1,), (1,)), ((), ())), preferred_element_type=F32)


def split(x):
    hi = x.astype(BF16)
    return hi, (x - hi.astype(F32)).astype(BF16)


def both(op, a, w):
    rows = a[0].shape[0]
    out = op(jnp.concatenate(a, 0), w)
    return out[:rows] + out[rows:]


def three(op, a, b):
    return both(op, a, b[0]) + op(a[0], b[1])


def iota(shape, dim):
    return lax.broadcasted_iota(jnp.int32, shape, dim)


def low_lane(shape):
    return lax.rem(iota(shape, 1), LANES) < HALF


def diagonal(shape):
    return (lax.rem(iota(shape, 0), LANES) < HALF) == low_lane(shape)


def swap(x):
    return jnp.concatenate([x[HALF:], x[:HALF]], 0)


def pack(d):
    return jnp.where(diagonal((LANES, LANES)), d[:, :LANES], swap(d[:, LANES:]))


def unpack(x):
    diag = diagonal((LANES, LANES))
    return jnp.concatenate([jnp.where(diag, x, 0.0), jnp.where(diag, swap(x), 0.0)], 1)


def stacked(x):
    low = low_lane(x.shape)
    zero = jnp.zeros_like(x)
    return jnp.concatenate([jnp.where(low, x, zero), jnp.where(low, zero, x)], 0)


def side_by_side(x):
    return jnp.concatenate([x[:BLOCK], x[BLOCK:]], 1)


def block_ones():
    return jnp.where(diagonal((LANES, LANES)), 1.0, 0.0).astype(BF16)


def head_sum(x):
    return both(nn, split(x), block_ones())


def block_maps(maps_ref):
    twice = jnp.where(
        iota((HALF, LANES), 0) == lax.rem(iota((HALF, LANES), 1), HALF), 1.0, 0.0
    ).astype(BF16)
    wide = nn(maps_ref[...], twice)
    return jnp.where(diagonal(wide.shape), wide, 0.0).astype(BF16)


def cols(p, width=LANES):
    return slice(p * width, (p + 1) * width)


def softmaxes(z):
    low = low_lane(z.shape)
    inf = jnp.inf
    top = jnp.where(
        low,
        jnp.max(jnp.where(low, z, -inf), 1, keepdims=True),
        jnp.max(jnp.where(low, -inf, z), 1, keepdims=True),
    )
    bottom = jnp.where(
        low,
        jnp.min(jnp.where(low, z, inf), 1, keepdims=True),
        jnp.min(jnp.where(low, inf, z), 1, keepdims=True),
    )
    up = jnp.exp(z - top)
    down = jnp.exp(bottom - z)
    return up / head_sum(up), down / head_sum(down)


def core():
    return lax.axis_index("core")


def chip(sizes):
    return lax.axis_index("z") * sizes["x"] + lax.axis_index("x")


def causal(rows):
    return iota((rows, BLOCK), 1) <= lax.rem(iota((rows, BLOCK), 0), BLOCK)


def causal_back(rows):
    return iota((rows, BLOCK), 1) >= lax.rem(iota((rows, BLOCK), 0), BLOCK)


def start_kernel(a, b, maps, send, own, wide, other, few, sems):
    mine = pl.ds(pl.multiple_of(core() * WIDE, WIDE), WIDE)
    theirs = pl.ds(pl.multiple_of((1 - core()) * WIDE, WIDE), WIDE)
    copies = []
    for i, ref in enumerate((a, b)):
        here = pl.ds(i * WIDE, WIDE)
        copies.append(pltpu.make_async_copy(ref.at[:, theirs], other.at[:, here], sems.at[2 * i]))
        copies.append(pltpu.make_async_copy(ref.at[:, mine], own.at[:, here], sems.at[2 * i + 1]))
    copies.append(pltpu.make_async_copy(maps.at[mine, :], few, sems.at[4]))
    for copy in copies:
        copy.start()
    copies[4].wait()
    wide[...] = block_maps(few)
    for copy in copies[:4]:
        copy.wait()
    send[...] = other[...].astype(F32)


def assemble(own, got, first, second):
    here = pl.ds(pl.multiple_of(core() * TOK, TOK), TOK)
    there = pl.ds(pl.multiple_of((1 - core()) * TOK, TOK), TOK)
    for i, ref in enumerate((first, second)):
        lanes = slice(i * WIDE, (i + 1) * WIDE)
        ref[here, :] = own[:, lanes]
        ref[there, :] = got[1 - core(), :, lanes].astype(BF16)


def keys_kernel(own, got, wk, send, k, v, kh, kl):
    assemble(own, got, k, v)
    chips = send.shape[0]
    rows = WIDE // chips
    state, sums_p, sums_m = [], [], []
    for p in range(PAIRS):
        c = cols(p)
        pk, mk = softmaxes(nn(k[:, c], wk[c]))
        sums_p.append(jnp.sum(pk, 0, keepdims=True))
        sums_m.append(jnp.sum(mk, 0, keepdims=True))
        hi, lo = split(jnp.concatenate([pk, mk], 1))
        kh[:, cols(p, 2 * LANES)] = hi
        kl[:, cols(p, 2 * LANES)] = lo
        vt = v[:, c].T
        state.append(pack(nn(vt, hi) + nn(vt, lo)))
    send[:, :rows, :] = jnp.concatenate(state, 0).reshape(chips, rows, LANES)
    sums = jnp.concatenate(sums_p + sums_m + [jnp.zeros((4, LANES), F32)], 0)
    send[:, rows:, :] = jnp.broadcast_to(sums[None], (chips, 8, LANES))


def queries_kernel(own, got, wq, v, kh, kl, q, g, qh, ql, num, den):
    assemble(own, got, q, g)
    mask = causal(2 * BLOCK)
    for p in range(PAIRS):
        c = cols(p)
        w = cols(p, 2 * LANES)
        pq, mq = softmaxes(nn(q[:, c], wq[c]))
        q2 = split(jnp.concatenate([pq, mq], 1))
        qh[:, w], ql[:, w] = q2
        k2 = (kh[:, w], kl[:, w])
        scores = three(nt, (stacked(q2[0]), stacked(q2[1])), k2)
        scores = side_by_side(jnp.where(mask, scores, 0.0))
        v2 = stacked(v[:, c])
        ones = stacked(jnp.ones((BLOCK, LANES), BF16))
        out = both(nn, split(scores), jnp.concatenate([v2, ones], 1))
        num[:, c] = out[:, :LANES]
        den[:, c] = out[:, LANES:]


def second_kernel(sizes, got, g, qh, ql, denl, send, den, dn, ksum):
    chips = send.shape[0]
    rows = WIDE // chips
    me = chip(sizes)
    acc = jnp.zeros((8, LANES), F32)
    run = jnp.zeros((rows, LANES), F32)
    for m in range(chips):
        send[m, :rows, :] = run
        run = run + got[m, :rows, :]
        acc = acc + jnp.where(m < me, got[m, rows:, :], 0.0)
    ksum[...] = acc
    diag = diagonal((LANES, 2 * LANES))
    out = []
    for p in range(PAIRS):
        c = cols(p)
        w = cols(p, 2 * LANES)
        q2 = (qh[:, w], ql[:, w])
        sums = jnp.concatenate([acc[p : p + 1], acc[p + PAIRS : p + PAIRS + 1]], 1)
        sums = jnp.where(diag, jnp.broadcast_to(sums, (LANES, 2 * LANES)), 0.0)
        d = denl[:, c] + three(nt, q2, split(sums))
        den[:, c] = d
        scaled = g[:, c].astype(F32) / d
        dn[:, c] = scaled
        out.append(pack(three(nn, split(scaled.T), q2)))
    send[:, rows:, :] = jnp.concatenate(out, 0).reshape(chips, rows, LANES)


def local_kernel(v, qh, ql, kh, kl, dn, gql, gvl, token):
    token[...] = jnp.zeros_like(token)
    mask = causal(2 * BLOCK)
    back_mask = causal_back(2 * BLOCK)
    for p in range(PAIRS):
        c = cols(p)
        w = cols(p, 2 * LANES)
        q2 = (qh[:, w], ql[:, w])
        k2 = (kh[:, w], kl[:, w])
        v2 = v[:, c]
        s2 = split(dn[:, c])
        d2 = (stacked(s2[0]), stacked(s2[1]))
        mixing = split(side_by_side(jnp.where(mask, both(nt, d2, v2), 0.0)))
        gql[:, w] = three(nn, mixing, (stacked(k2[0]), stacked(k2[1])))
        scores = three(nt, (stacked(k2[0]), stacked(k2[1])), q2)
        scores = split(side_by_side(jnp.where(back_mask, scores, 0.0)))
        gvl[:, c] = three(nn, scores, d2)


def third_kernel(got, g, qh, ql, numl, den, _, send, dd):
    chips = send.shape[0]
    rows = WIDE // chips
    run = jnp.zeros((rows, LANES), F32)
    for m in reversed(range(chips)):
        send[m, :rows, :] = run
        run = run + got[m, rows:, :]
    state = got[:, :rows, :].reshape(WIDE, LANES)
    sums_p, sums_m = [], []
    for p in range(PAIRS):
        c = cols(p)
        w = cols(p, 2 * LANES)
        q2 = (qh[:, w], ql[:, w])
        numer = numl[:, c] + three(nt, q2, split(unpack(state[c])))
        d = den[:, c]
        dden = -head_sum(g[:, c].astype(F32) * (numer / d)) / d
        dd[:, c] = dden
        full = q2[0].astype(F32) + q2[1].astype(F32)
        sums_p.append(jnp.sum(full[:, :LANES] * dden, 0, keepdims=True))
        sums_m.append(jnp.sum(full[:, LANES:] * dden, 0, keepdims=True))
    sums = jnp.concatenate(sums_p + sums_m + [jnp.zeros((4, LANES), F32)], 0)
    send[:, rows:, :] = jnp.broadcast_to(sums[None], (chips, 8, LANES))


def feature_back(f2, grad):
    full = f2[0].astype(F32) + f2[1].astype(F32)
    plus, minus = full[:, :LANES], full[:, LANES:]
    first, second = grad[:, :LANES], grad[:, LANES:]
    return plus * (first - head_sum(plus * first)) - minus * (second - head_sum(minus * second))


def twice(x):
    return jnp.concatenate([x, x], 1)


def fourth_kernel(got, q, v, wq, qh, ql, kh, kl, dn, dd, ksum, gql, whole, gq_map, gk_all):
    rows = WIDE // got.shape[0]
    state = got[:, :rows, :].reshape(WIDE, LANES)
    tri = jnp.where(causal(BLOCK), 1.0, 0.0).astype(BF16)
    tri_back = jnp.where(causal_back(BLOCK), 1.0, 0.0).astype(BF16)
    back_mask = causal_back(2 * BLOCK)
    for p in range(PAIRS):
        c = cols(p)
        w = cols(p, 2 * LANES)
        q2 = (qh[:, w], ql[:, w])
        dden = twice(dd[:, c])
        sums = jnp.concatenate([ksum[p : p + 1, :], ksum[p + PAIRS : p + PAIRS + 1, :]], 1)
        s2 = split(dn[:, c])
        grad = gql[:, w] + three(nn, s2, split(unpack(state[c])))
        grad = grad + dden * (sums + (nn(tri, kh[:, w]) + nn(tri, kl[:, w])))
        dzq = feature_back(q2, grad)
        z2 = split(dzq)
        whole[:, c] = both(nt, z2, wq[c])
        qt = q[:, c].T
        gq_map[c, :] = nn(qt, z2[0]) + nn(qt, z2[1])
        later = split((q2[0].astype(F32) + q2[1].astype(F32)) * dden)
        vv = stacked(v[:, c])
        back = jnp.where(back_mask, nt(vv, s2[0]) + nt(vv, s2[1]), 0.0)
        back = split(side_by_side(back))
        gk = three(nn, back, (stacked(q2[0]), stacked(q2[1])))
        gk_all[:, w] = gk + (nn(tri_back, later[0]) + nn(tri_back, later[1]))


def fifth_kernel(sizes, got, k, v, kh, kl, gkl, gq_map, send, dz):
    chips = send.shape[0]
    rows = WIDE // chips
    me = chip(sizes)
    acc = jnp.zeros((8, LANES), F32)
    for m in range(chips):
        acc = acc + jnp.where(m > me, got[m, rows:, :], 0.0)
    later = got[:, :rows, :].reshape(WIDE, LANES)
    out = []
    for p in range(PAIRS):
        c = cols(p)
        w = cols(p, 2 * LANES)
        k2 = (kh[:, w], kl[:, w])
        sums = jnp.concatenate([acc[p : p + 1], acc[p + PAIRS : p + PAIRS + 1]], 1)
        grad = gkl[:, w] + sums + nn(
            twice(v[:, c]), jnp.concatenate(split(unpack(later[c])), 0)
        )
        dzk = feature_back(k2, grad)
        dz[:, c] = dzk
        z2 = split(dzk)
        kt = k[:, c].T
        out.append(
            pack(jnp.concatenate([gq_map[c, :], nn(kt, z2[0]) + nn(kt, z2[1])], 1))
        )
    send[...] = jnp.concatenate(out, 0).reshape(chips, rows, LANES)


def sixth_kernel(got, wk, kh, kl, gvl, dz, whole):
    rows = WIDE // got.shape[0]
    later = got[:, :rows, :].reshape(WIDE, LANES)
    for p in range(PAIRS):
        c = cols(p)
        w = cols(p, 2 * LANES)
        whole[:, c] = both(nt, split(dz[:, c]), wk[c])
        grad = gvl[:, c] + three(nt, (kh[:, w], kl[:, w]), split(unpack(later[c])))
        whole[:, WIDE + p * LANES : WIDE + (p + 1) * LANES] = grad


def theirs_kernel(first, second, send):
    rows = pl.ds(pl.multiple_of((1 - core()) * TOK, TOK), TOK)
    send[:, :WIDE] = first[rows, :]
    send[:, WIDE:] = second[rows, :]


def finish_kernel(first, second, got, *outs):
    *outs, token = outs
    token[...] = jnp.zeros_like(token)
    rows = pl.ds(pl.multiple_of(core() * TOK, TOK), TOK)
    own = jnp.concatenate([first[rows, :], second[rows, :]], 1)
    other = got[1 - core()]
    zero = core() == 0
    for i, out in enumerate(outs):
        lanes = slice(i * WIDE, (i + 1) * WIDE)
        a, b = own[:, lanes], other[:, lanes]
        out[:, :WIDE] = jnp.where(zero, a, b).astype(BF16)
        out[:, WIDE:] = jnp.where(zero, b, a).astype(BF16)


def sum_kernel(got, *rest):
    send = rest[-1]
    total = got[0]
    for m in range(1, got.shape[0]):
        total = total + got[m]
    send[...] = jnp.broadcast_to(total[None], send.shape)


def sum_cores_kernel(got, send):
    acc = [got[0], got[1]]
    for m in range(2, got.shape[0]):
        acc[m % 2] = acc[m % 2] + got[m]
    send[...] = jnp.broadcast_to(jnp.concatenate(acc, 0)[None], send.shape)


def last_kernel(scale, got, gq, gk):
    rows = got.shape[1] // 2
    cores = [got[:, :rows, :].reshape(WIDE, LANES), got[:, rows:, :].reshape(WIDE, LANES)]
    for p in range(2 * PAIRS):
        x = cores[p // PAIRS][cols(p % PAIRS), :] * scale
        y = pltpu.roll(x, HALF, 1)
        gq[2 * p] = x[:HALF, :HALF].astype(BF16)
        gq[2 * p + 1] = y[HALF:, :HALF].astype(BF16)
        gk[2 * p] = x[HALF:, :HALF].astype(BF16)
        gk[2 * p + 1] = y[:HALF, :HALF].astype(BF16)


def call(kernel, outs, *args, flops=10**8, space=pltpu.VMEM, scratch=(), room=32):
    shapes = [jax.ShapeDtypeStruct(shape, dtype) for shape, dtype in outs]
    moved = sum(a.size * a.dtype.itemsize for a in (*args, *shapes))
    return pl.pallas_call(
        kernel,
        out_shape=shapes,
        in_specs=[pl.BlockSpec(memory_space=space)] * len(args),
        out_specs=[pl.BlockSpec(memory_space=pltpu.VMEM)] * len(outs),
        scratch_shapes=scratch,
        compiler_params=pltpu.CompilerParams(vmem_limit_bytes=int(room * 2**20)),
        cost_estimate=pl.CostEstimate(flops=flops, bytes_accessed=moved, transcendentals=0),
    )(*args)


def per_device(sizes, queries, keys, values, upstream, query_map, key_map):
    chips = sizes["z"] * sizes["x"]
    rows = WIDE // chips
    q, k, v, g = (a.reshape(TOK, 2 * WIDE) for a in (queries, keys, values, upstream))
    qmap = query_map.reshape(2 * WIDE, HALF)
    kmap = key_map.reshape(2 * WIDE, HALF)
    feats = ((BLOCK, 2 * WIDE), BF16)
    feats32 = ((BLOCK, 2 * WIDE), F32)
    flat = ((BLOCK, WIDE), F32)
    small = ((BLOCK, WIDE), BF16)
    sums = ((8, LANES), F32)

    def across(a):
        return lax.all_gather(a, "core")

    def exchange(a):
        return lax.all_to_all(a, CHIPS, 0, 0)

    def start(a, b, maps, room):
        send, own, wide = call(
            start_kernel,
            [((TOK, 2 * WIDE), F32), ((TOK, 2 * WIDE), BF16), ((WIDE, LANES), BF16)],
            a, b, maps,
            space=pl.ANY,
            room=room,
            scratch=[
                pltpu.VMEM((TOK, 2 * WIDE), BF16),
                pltpu.VMEM((WIDE, HALF), BF16),
                pltpu.SemaphoreType.DMA((5,)),
            ],
        )
        return own, across(send), wide

    own, got, wk = start(k, v, kmap, 60)
    send, k2, v2, kh, kl = call(
        keys_kernel, [((chips, rows + 8, LANES), F32), small, small, feats, feats], own, got, wk
    )
    first = exchange(send)
    own, got, wq = start(q, g, qmap, 32)
    q2, g2, qh, ql, numl, denl = call(
        queries_kernel,
        [small, small, feats, feats, flat, flat],
        own, got, wq, v2, kh, kl,
        flops=10**9,
    )
    send, den, dn, ksum = call(
        functools.partial(second_kernel, sizes),
        [((chips, 2 * rows, LANES), F32), flat, flat, sums],
        first, g2, qh, ql, denl,
    )
    second = exchange(send)
    gql, gvl, token = call(
        local_kernel, [feats32, flat, sums], v2, qh, ql, kh, kl, dn, flops=10**9
    )
    send, dd = call(
        third_kernel,
        [((chips, rows + 8, LANES), F32), flat],
        second, g2, qh, ql, numl, den, token,
    )
    third = exchange(send)
    whole_q, gq_map, gkl = call(
        fourth_kernel,
        [flat, ((WIDE, LANES), F32), feats32],
        second, q2, v2, wq, qh, ql, kh, kl, dn, dd, ksum, gql,
        flops=10**9,
    )
    send, dz = call(
        functools.partial(fifth_kernel, sizes),
        [((chips, rows, LANES), F32), flat],
        third, k2, v2, kh, kl, gkl, gq_map,
    )
    got = exchange(send)
    (whole,) = call(
        sixth_kernel, [((BLOCK, 2 * WIDE), F32)], third, wk, kh, kl, gvl, dz, flops=10**9
    )
    (send,) = call(theirs_kernel, [((TOK, 3 * WIDE), F32)], whole_q, whole)
    outs = [((TOK, 2 * WIDE), BF16)] * 3
    grad_q, grad_k, grad_v, token = call(
        finish_kernel, outs + [sums], whole_q, whole, across(send)
    )
    others = sizes["dp"] * sizes["core"]
    (send,) = call(sum_kernel, [((others, rows, LANES), F32)], got, token)
    got = lax.all_to_all(send, ("dp", "core"), 0, 0)
    (send,) = call(sum_cores_kernel, [((chips, 2 * rows, LANES), F32)], got)
    got = exchange(send)
    scale = float(BLOCK * chips * sizes["dp"]) ** (-0.5)
    heads = ((8, HALF, HALF), BF16)
    total_q, total_k = call(
        functools.partial(last_kernel, scale), [heads, heads], got
    )
    shape = queries.shape
    return grad_q.reshape(shape), grad_k.reshape(shape), grad_v.reshape(shape), total_q, total_k


def physical(mesh):
    dp, ctx = mesh.devices.shape
    x = 4 if ctx % 8 == 0 and ctx > 8 else 2
    sizes = {"dp": dp, "z": ctx // (2 * x), "x": x, "core": 2}
    return Mesh(mesh.devices.reshape(tuple(sizes.values())), tuple(sizes)), sizes


def solution(mesh):
    inner, sizes = physical(mesh)
    tokens = P("dp", CTX, None)
    return jax.shard_map(
        functools.partial(per_device, sizes),
        mesh=inner,
        in_specs=(tokens,) * 4 + (P(), P()),
        out_specs=(tokens,) * 3 + (P(), P()),
        check_vma=False,
    )
```

```python
import functools

import jax
import jax.numpy as jnp
import numpy as np
from jax import lax
from jax.experimental import pallas as pl
from jax.experimental.pallas import tpu as pltpu
from jax.sharding import Mesh, PartitionSpec as P

F32 = jnp.float32
BF16 = jnp.bfloat16
CTX = ("z", "x", "core")
CHIPS = ("z", "x")
LANES = 128
HALF = 64
TOK = 128
BLOCK = 256
PAIRS = 2
WIDE = PAIRS * LANES


def nn(a, b):
    return lax.dot_general(a, b, (((1,), (0,)), ((), ())), preferred_element_type=F32)


def nt(a, b):
    return lax.dot_general(a, b, (((1,), (1,)), ((), ())), preferred_element_type=F32)


def split(x):
    hi = x.astype(BF16)
    return hi, (x - hi.astype(F32)).astype(BF16)


def both(op, a, w):
    rows = a[0].shape[0]
    out = op(jnp.concatenate(a, 0), w)
    return out[:rows] + out[rows:]


def three(op, a, b):
    return both(op, a, b[0]) + op(a[0], b[1])


def iota(shape, dim):
    return lax.broadcasted_iota(jnp.int32, shape, dim)


def low_lane(shape):
    return lax.rem(iota(shape, 1), LANES) < HALF


def diagonal(shape):
    return (lax.rem(iota(shape, 0), LANES) < HALF) == low_lane(shape)


def swap(x):
    return jnp.concatenate([x[HALF:], x[:HALF]], 0)


def pack(d):
    return jnp.where(diagonal((LANES, LANES)), d[:, :LANES], swap(d[:, LANES:]))


def unpack(x):
    diag = diagonal((LANES, LANES))
    return jnp.concatenate([jnp.where(diag, x, 0.0), jnp.where(diag, swap(x), 0.0)], 1)


def stacked(x):
    low = low_lane(x.shape)
    zero = jnp.zeros_like(x)
    return jnp.concatenate([jnp.where(low, x, zero), jnp.where(low, zero, x)], 0)


def side_by_side(x):
    return jnp.concatenate([x[:BLOCK], x[BLOCK:]], 1)


def block_ones():
    return jnp.where(diagonal((LANES, LANES)), 1.0, 0.0).astype(BF16)


def head_sum(x):
    return both(nn, split(x), block_ones())


def block_maps(maps_ref):
    twice = jnp.where(
        iota((HALF, LANES), 0) == lax.rem(iota((HALF, LANES), 1), HALF), 1.0, 0.0
    ).astype(BF16)
    wide = nn(maps_ref[...], twice)
    return jnp.where(diagonal(wide.shape), wide, 0.0).astype(BF16)


def cols(p, width=LANES):
    return slice(p * width, (p + 1) * width)


def softmaxes(z):
    low = low_lane(z.shape)
    inf = jnp.inf
    top = jnp.where(
        low,
        jnp.max(jnp.where(low, z, -inf), 1, keepdims=True),
        jnp.max(jnp.where(low, -inf, z), 1, keepdims=True),
    )
    bottom = jnp.where(
        low,
        jnp.min(jnp.where(low, z, inf), 1, keepdims=True),
        jnp.min(jnp.where(low, inf, z), 1, keepdims=True),
    )
    up = jnp.exp(z - top)
    down = jnp.exp(bottom - z)
    return up / head_sum(up), down / head_sum(down)


def core():
    return lax.axis_index("core")


def chip(sizes):
    return lax.axis_index("z") * sizes["x"] + lax.axis_index("x")


def causal(rows):
    return iota((rows, BLOCK), 1) <= lax.rem(iota((rows, BLOCK), 0), BLOCK)


def causal_back(rows):
    return iota((rows, BLOCK), 1) >= lax.rem(iota((rows, BLOCK), 0), BLOCK)


def start_kernel(a, b, maps, send, own, wide, other, few, sems):
    mine = pl.ds(pl.multiple_of(core() * WIDE, WIDE), WIDE)
    theirs = pl.ds(pl.multiple_of((1 - core()) * WIDE, WIDE), WIDE)
    copies = []
    for i, ref in enumerate((a, b)):
        here = pl.ds(i * WIDE, WIDE)
        copies.append(pltpu.make_async_copy(ref.at[:, theirs], other.at[:, here], sems.at[2 * i]))
        copies.append(pltpu.make_async_copy(ref.at[:, mine], own.at[:, here], sems.at[2 * i + 1]))
    copies.append(pltpu.make_async_copy(maps.at[mine, :], few, sems.at[4]))
    for copy in copies:
        copy.start()
    copies[4].wait()
    wide[...] = block_maps(few)
    for copy in copies[:4]:
        copy.wait()
    send[...] = other[...].astype(F32)


def assemble(own, got, first, second):
    here = pl.ds(pl.multiple_of(core() * TOK, TOK), TOK)
    there = pl.ds(pl.multiple_of((1 - core()) * TOK, TOK), TOK)
    for i, ref in enumerate((first, second)):
        lanes = slice(i * WIDE, (i + 1) * WIDE)
        ref[here, :] = own[:, lanes]
        ref[there, :] = got[1 - core(), :, lanes].astype(BF16)


def keys_kernel(own, got, wk, send, k, v, kh, kl):
    assemble(own, got, k, v)
    chips = send.shape[0]
    rows = WIDE // chips
    state, sums_p, sums_m = [], [], []
    for p in range(PAIRS):
        c = cols(p)
        pk, mk = softmaxes(nn(k[:, c], wk[c]))
        sums_p.append(jnp.sum(pk, 0, keepdims=True))
        sums_m.append(jnp.sum(mk, 0, keepdims=True))
        hi, lo = split(jnp.concatenate([pk, mk], 1))
        kh[:, cols(p, 2 * LANES)] = hi
        kl[:, cols(p, 2 * LANES)] = lo
        vt = v[:, c].T
        state.append(pack(nn(vt, hi) + nn(vt, lo)))
    send[:, :rows, :] = jnp.concatenate(state, 0).reshape(chips, rows, LANES)
    sums = jnp.concatenate(sums_p + sums_m + [jnp.zeros((4, LANES), F32)], 0)
    send[:, rows:, :] = jnp.broadcast_to(sums[None], (chips, 8, LANES))


def queries_kernel(own, got, wq, v, kh, kl, q, g, qh, ql, num, den):
    assemble(own, got, q, g)
    mask = causal(2 * BLOCK)
    for p in range(PAIRS):
        c = cols(p)
        w = cols(p, 2 * LANES)
        pq, mq = softmaxes(nn(q[:, c], wq[c]))
        q2 = split(jnp.concatenate([pq, mq], 1))
        qh[:, w], ql[:, w] = q2
        k2 = (kh[:, w], kl[:, w])
        scores = three(nt, (stacked(q2[0]), stacked(q2[1])), k2)
        scores = side_by_side(jnp.where(mask, scores, 0.0))
        v2 = stacked(v[:, c])
        ones = stacked(jnp.ones((BLOCK, LANES), BF16))
        out = both(nn, split(scores), jnp.concatenate([v2, ones], 1))
        num[:, c] = out[:, :LANES]
        den[:, c] = out[:, LANES:]


def second_kernel(sizes, got, g, qh, ql, denl, send, den, dn, ksum):
    chips = send.shape[0]
    rows = WIDE // chips
    me = chip(sizes)
    acc = jnp.zeros((8, LANES), F32)
    run = jnp.zeros((rows, LANES), F32)
    for m in range(chips):
        send[m, :rows, :] = run
        run = run + got[m, :rows, :]
        acc = acc + jnp.where(m < me, got[m, rows:, :], 0.0)
    ksum[...] = acc
    diag = diagonal((LANES, 2 * LANES))
    out = []
    for p in range(PAIRS):
        c = cols(p)
        w = cols(p, 2 * LANES)
        q2 = (qh[:, w], ql[:, w])
        sums = jnp.concatenate([acc[p : p + 1], acc[p + PAIRS : p + PAIRS + 1]], 1)
        sums = jnp.where(diag, jnp.broadcast_to(sums, (LANES, 2 * LANES)), 0.0)
        d = denl[:, c] + three(nt, q2, split(sums))
        den[:, c] = d
        scaled = g[:, c].astype(F32) / d
        dn[:, c] = scaled
        out.append(pack(three(nn, split(scaled.T), q2)))
    send[:, rows:, :] = jnp.concatenate(out, 0).reshape(chips, rows, LANES)


def local_kernel(v, qh, ql, kh, kl, dn, gql, gvl, token):
    token[...] = jnp.zeros_like(token)
    mask = causal(2 * BLOCK)
    back_mask = causal_back(2 * BLOCK)
    for p in range(PAIRS):
        c = cols(p)
        w = cols(p, 2 * LANES)
        q2 = (qh[:, w], ql[:, w])
        k2 = (kh[:, w], kl[:, w])
        v2 = v[:, c]
        s2 = split(dn[:, c])
        d2 = (stacked(s2[0]), stacked(s2[1]))
        mixing = split(side_by_side(jnp.where(mask, both(nt, d2, v2), 0.0)))
        gql[:, w] = three(nn, mixing, (stacked(k2[0]), stacked(k2[1])))
        scores = three(nt, (stacked(k2[0]), stacked(k2[1])), q2)
        scores = split(side_by_side(jnp.where(back_mask, scores, 0.0)))
        gvl[:, c] = three(nn, scores, d2)


def third_kernel(got, g, qh, ql, numl, den, _, send, dd):
    chips = send.shape[0]
    rows = WIDE // chips
    run = jnp.zeros((rows, LANES), F32)
    for m in reversed(range(chips)):
        send[m, :rows, :] = run
        run = run + got[m, rows:, :]
    state = got[:, :rows, :].reshape(WIDE, LANES)
    sums_p, sums_m = [], []
    for p in range(PAIRS):
        c = cols(p)
        w = cols(p, 2 * LANES)
        q2 = (qh[:, w], ql[:, w])
        numer = numl[:, c] + three(nt, q2, split(unpack(state[c])))
        d = den[:, c]
        dden = -head_sum(g[:, c].astype(F32) * (numer / d)) / d
        dd[:, c] = dden
        full = q2[0].astype(F32) + q2[1].astype(F32)
        sums_p.append(jnp.sum(full[:, :LANES] * dden, 0, keepdims=True))
        sums_m.append(jnp.sum(full[:, LANES:] * dden, 0, keepdims=True))
    sums = jnp.concatenate(sums_p + sums_m + [jnp.zeros((4, LANES), F32)], 0)
    send[:, rows:, :] = jnp.broadcast_to(sums[None], (chips, 8, LANES))


def feature_back(f2, grad):
    full = f2[0].astype(F32) + f2[1].astype(F32)
    plus, minus = full[:, :LANES], full[:, LANES:]
    first, second = grad[:, :LANES], grad[:, LANES:]
    return plus * (first - head_sum(plus * first)) - minus * (second - head_sum(minus * second))


def twice(x):
    return jnp.concatenate([x, x], 1)


def fourth_kernel(got, q, v, wq, qh, ql, kh, kl, dn, dd, ksum, gql, whole, gq_map, gk_all):
    rows = WIDE // got.shape[0]
    state = got[:, :rows, :].reshape(WIDE, LANES)
    tri = jnp.where(causal(BLOCK), 1.0, 0.0).astype(BF16)
    tri_back = jnp.where(causal_back(BLOCK), 1.0, 0.0).astype(BF16)
    back_mask = causal_back(2 * BLOCK)
    for p in range(PAIRS):
        c = cols(p)
        w = cols(p, 2 * LANES)
        q2 = (qh[:, w], ql[:, w])
        dden = twice(dd[:, c])
        sums = jnp.concatenate([ksum[p : p + 1, :], ksum[p + PAIRS : p + PAIRS + 1, :]], 1)
        s2 = split(dn[:, c])
        grad = gql[:, w] + three(nn, s2, split(unpack(state[c])))
        grad = grad + dden * (sums + (nn(tri, kh[:, w]) + nn(tri, kl[:, w])))
        dzq = feature_back(q2, grad)
        z2 = split(dzq)
        whole[:, c] = both(nt, z2, wq[c])
        qt = q[:, c].T
        gq_map[c, :] = nn(qt, z2[0]) + nn(qt, z2[1])
        later = split((q2[0].astype(F32) + q2[1].astype(F32)) * dden)
        vv = stacked(v[:, c])
        back = jnp.where(back_mask, nt(vv, s2[0]) + nt(vv, s2[1]), 0.0)
        back = split(side_by_side(back))
        gk = three(nn, back, (stacked(q2[0]), stacked(q2[1])))
        gk_all[:, w] = gk + (nn(tri_back, later[0]) + nn(tri_back, later[1]))


def fifth_kernel(sizes, got, k, v, kh, kl, gkl, gq_map, send, dz):
    chips = send.shape[0]
    rows = WIDE // chips
    me = chip(sizes)
    acc = jnp.zeros((8, LANES), F32)
    for m in range(chips):
        acc = acc + jnp.where(m > me, got[m, rows:, :], 0.0)
    later = got[:, :rows, :].reshape(WIDE, LANES)
    out = []
    for p in range(PAIRS):
        c = cols(p)
        w = cols(p, 2 * LANES)
        k2 = (kh[:, w], kl[:, w])
        sums = jnp.concatenate([acc[p : p + 1], acc[p + PAIRS : p + PAIRS + 1]], 1)
        grad = gkl[:, w] + sums + nn(
            twice(v[:, c]), jnp.concatenate(split(unpack(later[c])), 0)
        )
        dzk = feature_back(k2, grad)
        dz[:, c] = dzk
        z2 = split(dzk)
        kt = k[:, c].T
        out.append(
            pack(jnp.concatenate([gq_map[c, :], nn(kt, z2[0]) + nn(kt, z2[1])], 1))
        )
    send[...] = jnp.concatenate(out, 0).reshape(chips, rows, LANES)


def sixth_kernel(got, wk, kh, kl, gvl, dz, whole):
    rows = WIDE // got.shape[0]
    later = got[:, :rows, :].reshape(WIDE, LANES)
    for p in range(PAIRS):
        c = cols(p)
        w = cols(p, 2 * LANES)
        whole[:, c] = both(nt, split(dz[:, c]), wk[c])
        grad = gvl[:, c] + three(nt, (kh[:, w], kl[:, w]), split(unpack(later[c])))
        whole[:, WIDE + p * LANES : WIDE + (p + 1) * LANES] = grad


def theirs_kernel(first, second, send):
    rows = pl.ds(pl.multiple_of((1 - core()) * TOK, TOK), TOK)
    send[:, :WIDE] = first[rows, :]
    send[:, WIDE:] = second[rows, :]


def finish_kernel(first, second, got, *outs):
    *outs, token = outs
    token[...] = jnp.zeros_like(token)
    rows = pl.ds(pl.multiple_of(core() * TOK, TOK), TOK)
    own = jnp.concatenate([first[rows, :], second[rows, :]], 1)
    other = got[1 - core()]
    zero = core() == 0
    for i, out in enumerate(outs):
        lanes = slice(i * WIDE, (i + 1) * WIDE)
        a, b = own[:, lanes], other[:, lanes]
        out[:, :WIDE] = jnp.where(zero, a, b).astype(BF16)
        out[:, WIDE:] = jnp.where(zero, b, a).astype(BF16)


def sum_kernel(got, *rest):
    send = rest[-1]
    total = got[0]
    for m in range(1, got.shape[0]):
        total = total + got[m]
    send[...] = jnp.broadcast_to(total[None], send.shape)


def sum_cores_kernel(got, send):
    acc = [got[0], got[1]]
    for m in range(2, got.shape[0]):
        acc[m % 2] = acc[m % 2] + got[m]
    send[...] = jnp.broadcast_to(jnp.concatenate(acc, 0)[None], send.shape)


def last_kernel(scale, got, gq, gk):
    rows = got.shape[1] // 2
    cores = [got[:, :rows, :].reshape(WIDE, LANES), got[:, rows:, :].reshape(WIDE, LANES)]
    for p in range(2 * PAIRS):
        x = cores[p // PAIRS][cols(p % PAIRS), :] * scale
        y = pltpu.roll(x, HALF, 1)
        gq[2 * p] = x[:HALF, :HALF].astype(BF16)
        gq[2 * p + 1] = y[HALF:, :HALF].astype(BF16)
        gk[2 * p] = x[HALF:, :HALF].astype(BF16)
        gk[2 * p + 1] = y[:HALF, :HALF].astype(BF16)


def call(kernel, outs, *args, flops=10**8, space=pltpu.VMEM, scratch=(), room=32):
    shapes = [jax.ShapeDtypeStruct(shape, dtype) for shape, dtype in outs]
    moved = sum(a.size * a.dtype.itemsize for a in (*args, *shapes))
    return pl.pallas_call(
        kernel,
        out_shape=shapes,
        in_specs=[pl.BlockSpec(memory_space=space)] * len(args),
        out_specs=[pl.BlockSpec(memory_space=pltpu.VMEM)] * len(outs),
        scratch_shapes=scratch,
        compiler_params=pltpu.CompilerParams(vmem_limit_bytes=int(room * 2**20)),
        cost_estimate=pl.CostEstimate(flops=flops, bytes_accessed=moved, transcendentals=0),
    )(*args)


def per_device(sizes, queries, keys, values, upstream, query_map, key_map):
    chips = sizes["z"] * sizes["x"]
    rows = WIDE // chips
    q, k, v, g = (a.reshape(TOK, 2 * WIDE) for a in (queries, keys, values, upstream))
    qmap = query_map.reshape(2 * WIDE, HALF)
    kmap = key_map.reshape(2 * WIDE, HALF)
    feats = ((BLOCK, 2 * WIDE), BF16)
    feats32 = ((BLOCK, 2 * WIDE), F32)
    flat = ((BLOCK, WIDE), F32)
    small = ((BLOCK, WIDE), BF16)
    sums = ((8, LANES), F32)

    def across(a):
        return lax.all_gather(a, "core")

    def exchange(a):
        return lax.all_to_all(a, CHIPS, 0, 0)

    def start(a, b, maps, room):
        send, own, wide = call(
            start_kernel,
            [((TOK, 2 * WIDE), F32), ((TOK, 2 * WIDE), BF16), ((WIDE, LANES), BF16)],
            a, b, maps,
            space=pl.ANY,
            room=room,
            scratch=[
                pltpu.VMEM((TOK, 2 * WIDE), BF16),
                pltpu.VMEM((WIDE, HALF), BF16),
                pltpu.SemaphoreType.DMA((5,)),
            ],
        )
        return own, across(send), wide

    own, got, wk = start(k, v, kmap, 60)
    send, k2, v2, kh, kl = call(
        keys_kernel, [((chips, rows + 8, LANES), F32), small, small, feats, feats], own, got, wk
    )
    first = exchange(send)
    own, got, wq = start(q, g, qmap, 32)
    q2, g2, qh, ql, numl, denl = call(
        queries_kernel,
        [small, small, feats, feats, flat, flat],
        own, got, wq, v2, kh, kl,
        flops=10**9,
    )
    send, den, dn, ksum = call(
        functools.partial(second_kernel, sizes),
        [((chips, 2 * rows, LANES), F32), flat, flat, sums],
        first, g2, qh, ql, denl,
    )
    second = exchange(send)
    gql, gvl, token = call(
        local_kernel, [feats32, flat, sums], v2, qh, ql, kh, kl, dn, flops=10**9
    )
    send, dd = call(
        third_kernel,
        [((chips, rows + 8, LANES), F32), flat],
        second, g2, qh, ql, numl, den, token,
    )
    third = exchange(send)
    whole_q, gq_map, gkl = call(
        fourth_kernel,
        [flat, ((WIDE, LANES), F32), feats32],
        second, q2, v2, wq, qh, ql, kh, kl, dn, dd, ksum, gql,
        flops=10**9,
    )
    send, dz = call(
        functools.partial(fifth_kernel, sizes),
        [((chips, rows, LANES), F32), flat],
        third, k2, v2, kh, kl, gkl, gq_map,
    )
    got = exchange(send)
    (whole,) = call(
        sixth_kernel, [((BLOCK, 2 * WIDE), F32)], third, wk, kh, kl, gvl, dz, flops=10**9
    )
    (send,) = call(theirs_kernel, [((TOK, 3 * WIDE), F32)], whole_q, whole)
    outs = [((TOK, 2 * WIDE), BF16)] * 3
    grad_q, grad_k, grad_v, token = call(
        finish_kernel, outs + [sums], whole_q, whole, across(send)
    )
    others = sizes["dp"] * sizes["core"]
    (send,) = call(sum_kernel, [((others, rows, LANES), F32)], got, send)
    got = lax.all_to_all(send, ("dp", "core"), 0, 0)
    (send,) = call(sum_cores_kernel, [((chips, 2 * rows, LANES), F32)], got)
    got = exchange(send)
    scale = float(BLOCK * chips * sizes["dp"]) ** (-0.5)
    heads = ((8, HALF, HALF), BF16)
    total_q, total_k = call(
        functools.partial(last_kernel, scale), [heads, heads], got
    )
    shape = queries.shape
    return grad_q.reshape(shape), grad_k.reshape(shape), grad_v.reshape(shape), total_q, total_k


def physical(mesh):
    dp, ctx = mesh.devices.shape
    x = 4 if ctx % 8 == 0 and ctx > 8 else 2
    sizes = {"dp": dp, "z": ctx // (2 * x), "x": x, "core": 2}
    return Mesh(mesh.devices.reshape(tuple(sizes.values())), tuple(sizes)), sizes


def solution(mesh):
    inner, sizes = physical(mesh)
    tokens = P("dp", CTX, None)
    return jax.shard_map(
        functools.partial(per_device, sizes),
        mesh=inner,
        in_specs=(tokens,) * 4 + (P(), P()),
        out_specs=(tokens,) * 3 + (P(), P()),
        check_vma=False,
    )
```

```python
import functools

import jax
import jax.numpy as jnp
import numpy as np
from jax import lax
from jax.experimental import pallas as pl
from jax.experimental.pallas import tpu as pltpu
from jax.sharding import Mesh, PartitionSpec as P

F32 = jnp.float32
BF16 = jnp.bfloat16
CTX = ("z", "x", "core")
CHIPS = ("z", "x")
LANES = 128
HALF = 64
TOK = 128
BLOCK = 256
PAIRS = 2
WIDE = PAIRS * LANES


def nn(a, b):
    return lax.dot_general(a, b, (((1,), (0,)), ((), ())), preferred_element_type=F32)


def nt(a, b):
    return lax.dot_general(a, b, (((1,), (1,)), ((), ())), preferred_element_type=F32)


def split(x):
    hi = x.astype(BF16)
    return hi, (x - hi.astype(F32)).astype(BF16)


def both(op, a, w):
    rows = a[0].shape[0]
    out = op(jnp.concatenate(a, 0), w)
    return out[:rows] + out[rows:]


def three(op, a, b):
    return both(op, a, b[0]) + op(a[0], b[1])


def iota(shape, dim):
    return lax.broadcasted_iota(jnp.int32, shape, dim)


def low_lane(shape):
    return lax.rem(iota(shape, 1), LANES) < HALF


def diagonal(shape):
    return (lax.rem(iota(shape, 0), LANES) < HALF) == low_lane(shape)


def swap(x):
    return jnp.concatenate([x[HALF:], x[:HALF]], 0)


def pack(d):
    return jnp.where(diagonal((LANES, LANES)), d[:, :LANES], swap(d[:, LANES:]))


def unpack(x):
    diag = diagonal((LANES, LANES))
    return jnp.concatenate([jnp.where(diag, x, 0.0), jnp.where(diag, swap(x), 0.0)], 1)


def stacked(x):
    low = low_lane(x.shape)
    zero = jnp.zeros_like(x)
    return jnp.concatenate([jnp.where(low, x, zero), jnp.where(low, zero, x)], 0)


def side_by_side(x):
    return jnp.concatenate([x[:BLOCK], x[BLOCK:]], 1)


def block_ones():
    return jnp.where(diagonal((LANES, LANES)), 1.0, 0.0).astype(BF16)


def head_sum(x):
    return both(nn, split(x), block_ones())


def block_maps(maps_ref):
    twice = jnp.where(
        iota((HALF, LANES), 0) == lax.rem(iota((HALF, LANES), 1), HALF), 1.0, 0.0
    ).astype(BF16)
    wide = nn(maps_ref[...], twice)
    return jnp.where(diagonal(wide.shape), wide, 0.0).astype(BF16)


def cols(p, width=LANES):
    return slice(p * width, (p + 1) * width)


def softmaxes(z):
    low = low_lane(z.shape)
    inf = jnp.inf
    top = jnp.where(
        low,
        jnp.max(jnp.where(low, z, -inf), 1, keepdims=True),
        jnp.max(jnp.where(low, -inf, z), 1, keepdims=True),
    )
    bottom = jnp.where(
        low,
        jnp.min(jnp.where(low, z, inf), 1, keepdims=True),
        jnp.min(jnp.where(low, inf, z), 1, keepdims=True),
    )
    up = jnp.exp(z - top)
    down = jnp.exp(bottom - z)
    return up / head_sum(up), down / head_sum(down)


def core():
    return lax.axis_index("core")


def chip(sizes):
    return lax.axis_index("z") * sizes["x"] + lax.axis_index("x")


def causal(rows):
    return iota((rows, BLOCK), 1) <= lax.rem(iota((rows, BLOCK), 0), BLOCK)


def causal_back(rows):
    return iota((rows, BLOCK), 1) >= lax.rem(iota((rows, BLOCK), 0), BLOCK)


def start_kernel(a, b, maps, send, own, wide, other, few, sems):
    mine = pl.ds(pl.multiple_of(core() * WIDE, WIDE), WIDE)
    theirs = pl.ds(pl.multiple_of((1 - core()) * WIDE, WIDE), WIDE)
    copies = []
    for i, ref in enumerate((a, b)):
        here = pl.ds(i * WIDE, WIDE)
        copies.append(pltpu.make_async_copy(ref.at[:, theirs], other.at[:, here], sems.at[2 * i]))
        copies.append(pltpu.make_async_copy(ref.at[:, mine], own.at[:, here], sems.at[2 * i + 1]))
    copies.append(pltpu.make_async_copy(maps.at[mine, :], few, sems.at[4]))
    for copy in copies:
        copy.start()
    copies[4].wait()
    wide[...] = block_maps(few)
    for copy in copies[:4]:
        copy.wait()
    send[...] = other[...].astype(F32)


def assemble(own, got, first, second):
    here = pl.ds(pl.multiple_of(core() * TOK, TOK), TOK)
    there = pl.ds(pl.multiple_of((1 - core()) * TOK, TOK), TOK)
    for i, ref in enumerate((first, second)):
        lanes = slice(i * WIDE, (i + 1) * WIDE)
        ref[here, :] = own[:, lanes]
        ref[there, :] = got[1 - core(), :, lanes].astype(BF16)


def keys_kernel(own, got, wk, send, k, v, kh, kl):
    assemble(own, got, k, v)
    chips = send.shape[0]
    rows = WIDE // chips
    state, sums_p, sums_m = [], [], []
    for p in range(PAIRS):
        c = cols(p)
        pk, mk = softmaxes(nn(k[:, c], wk[c]))
        sums_p.append(jnp.sum(pk, 0, keepdims=True))
        sums_m.append(jnp.sum(mk, 0, keepdims=True))
        hi, lo = split(jnp.concatenate([pk, mk], 1))
        kh[:, cols(p, 2 * LANES)] = hi
        kl[:, cols(p, 2 * LANES)] = lo
        vt = v[:, c].T
        state.append(pack(nn(vt, hi) + nn(vt, lo)))
    send[:, :rows, :] = jnp.concatenate(state, 0).reshape(chips, rows, LANES)
    sums = jnp.concatenate(sums_p + sums_m + [jnp.zeros((4, LANES), F32)], 0)
    send[:, rows:, :] = jnp.broadcast_to(sums[None], (chips, 8, LANES))


def queries_kernel(own, got, wq, v, kh, kl, q, g, qh, ql, num, den):
    assemble(own, got, q, g)
    mask = causal(2 * BLOCK)
    for p in range(PAIRS):
        c = cols(p)
        w = cols(p, 2 * LANES)
        pq, mq = softmaxes(nn(q[:, c], wq[c]))
        q2 = split(jnp.concatenate([pq, mq], 1))
        qh[:, w], ql[:, w] = q2
        k2 = (kh[:, w], kl[:, w])
        scores = three(nt, (stacked(q2[0]), stacked(q2[1])), k2)
        scores = side_by_side(jnp.where(mask, scores, 0.0))
        v2 = stacked(v[:, c])
        ones = stacked(jnp.ones((BLOCK, LANES), BF16))
        out = both(nn, split(scores), jnp.concatenate([v2, ones], 1))
        num[:, c] = out[:, :LANES]
        den[:, c] = out[:, LANES:]


def second_kernel(sizes, got, g, qh, ql, denl, send, den, dn, ksum):
    chips = send.shape[0]
    rows = WIDE // chips
    me = chip(sizes)
    acc = jnp.zeros((8, LANES), F32)
    run = jnp.zeros((rows, LANES), F32)
    for m in range(chips):
        send[m, :rows, :] = run
        run = run + got[m, :rows, :]
        acc = acc + jnp.where(m < me, got[m, rows:, :], 0.0)
    ksum[...] = acc
    diag = diagonal((LANES, 2 * LANES))
    out = []
    for p in range(PAIRS):
        c = cols(p)
        w = cols(p, 2 * LANES)
        q2 = (qh[:, w], ql[:, w])
        sums = jnp.concatenate([acc[p : p + 1], acc[p + PAIRS : p + PAIRS + 1]], 1)
        sums = jnp.where(diag, jnp.broadcast_to(sums, (LANES, 2 * LANES)), 0.0)
        d = denl[:, c] + three(nt, q2, split(sums))
        den[:, c] = d
        scaled = g[:, c].astype(F32) / d
        dn[:, c] = scaled
        out.append(pack(three(nn, split(scaled.T), q2)))
    send[:, rows:, :] = jnp.concatenate(out, 0).reshape(chips, rows, LANES)


def local_kernel(v, qh, ql, kh, kl, dn, gql, gvl, token):
    token[...] = jnp.zeros_like(token)
    mask = causal(2 * BLOCK)
    back_mask = causal_back(2 * BLOCK)
    for p in range(PAIRS):
        c = cols(p)
        w = cols(p, 2 * LANES)
        q2 = (qh[:, w], ql[:, w])
        k2 = (kh[:, w], kl[:, w])
        v2 = v[:, c]
        s2 = split(dn[:, c])
        d2 = (stacked(s2[0]), stacked(s2[1]))
        mixing = split(side_by_side(jnp.where(mask, both(nt, d2, v2), 0.0)))
        gql[:, w] = three(nn, mixing, (stacked(k2[0]), stacked(k2[1])))
        scores = three(nt, (stacked(k2[0]), stacked(k2[1])), q2)
        scores = split(side_by_side(jnp.where(back_mask, scores, 0.0)))
        gvl[:, c] = three(nn, scores, d2)


def third_kernel(got, g, qh, ql, numl, den, _, send, dd):
    chips = send.shape[0]
    rows = WIDE // chips
    run = jnp.zeros((rows, LANES), F32)
    for m in reversed(range(chips)):
        send[m, :rows, :] = run
        run = run + got[m, rows:, :]
    state = got[:, :rows, :].reshape(WIDE, LANES)
    sums_p, sums_m = [], []
    for p in range(PAIRS):
        c = cols(p)
        w = cols(p, 2 * LANES)
        q2 = (qh[:, w], ql[:, w])
        numer = numl[:, c] + three(nt, q2, split(unpack(state[c])))
        d = den[:, c]
        dden = -head_sum(g[:, c].astype(F32) * (numer / d)) / d
        dd[:, c] = dden
        full = q2[0].astype(F32) + q2[1].astype(F32)
        sums_p.append(jnp.sum(full[:, :LANES] * dden, 0, keepdims=True))
        sums_m.append(jnp.sum(full[:, LANES:] * dden, 0, keepdims=True))
    sums = jnp.concatenate(sums_p + sums_m + [jnp.zeros((4, LANES), F32)], 0)
    send[:, rows:, :] = jnp.broadcast_to(sums[None], (chips, 8, LANES))


def feature_back(f2, grad):
    full = f2[0].astype(F32) + f2[1].astype(F32)
    plus, minus = full[:, :LANES], full[:, LANES:]
    first, second = grad[:, :LANES], grad[:, LANES:]
    return plus * (first - head_sum(plus * first)) - minus * (second - head_sum(minus * second))


def twice(x):
    return jnp.concatenate([x, x], 1)


def fourth_kernel(got, q, v, wq, qh, ql, kh, kl, dn, dd, ksum, gql, whole, gq_map, gk_all):
    rows = WIDE // got.shape[0]
    state = got[:, :rows, :].reshape(WIDE, LANES)
    tri = jnp.where(causal(BLOCK), 1.0, 0.0).astype(BF16)
    tri_back = jnp.where(causal_back(BLOCK), 1.0, 0.0).astype(BF16)
    back_mask = causal_back(2 * BLOCK)
    for p in range(PAIRS):
        c = cols(p)
        w = cols(p, 2 * LANES)
        q2 = (qh[:, w], ql[:, w])
        dden = twice(dd[:, c])
        sums = jnp.concatenate([ksum[p : p + 1, :], ksum[p + PAIRS : p + PAIRS + 1, :]], 1)
        s2 = split(dn[:, c])
        grad = gql[:, w] + three(nn, s2, split(unpack(state[c])))
        grad = grad + dden * (sums + (nn(tri, kh[:, w]) + nn(tri, kl[:, w])))
        dzq = feature_back(q2, grad)
        z2 = split(dzq)
        whole[:, c] = both(nt, z2, wq[c])
        qt = q[:, c].T
        gq_map[c, :] = nn(qt, z2[0]) + nn(qt, z2[1])
        later = split((q2[0].astype(F32) + q2[1].astype(F32)) * dden)
        vv = stacked(v[:, c])
        back = jnp.where(back_mask, nt(vv, s2[0]) + nt(vv, s2[1]), 0.0)
        back = split(side_by_side(back))
        gk = three(nn, back, (stacked(q2[0]), stacked(q2[1])))
        gk_all[:, w] = gk + (nn(tri_back, later[0]) + nn(tri_back, later[1]))


def fifth_kernel(sizes, got, k, v, kh, kl, gkl, gq_map, send, dz):
    chips = send.shape[0]
    rows = WIDE // chips
    me = chip(sizes)
    acc = jnp.zeros((8, LANES), F32)
    for m in range(chips):
        acc = acc + jnp.where(m > me, got[m, rows:, :], 0.0)
    later = got[:, :rows, :].reshape(WIDE, LANES)
    out = []
    for p in range(PAIRS):
        c = cols(p)
        w = cols(p, 2 * LANES)
        k2 = (kh[:, w], kl[:, w])
        sums = jnp.concatenate([acc[p : p + 1], acc[p + PAIRS : p + PAIRS + 1]], 1)
        grad = gkl[:, w] + sums + nn(
            twice(v[:, c]), jnp.concatenate(split(unpack(later[c])), 0)
        )
        dzk = feature_back(k2, grad)
        dz[:, c] = dzk
        z2 = split(dzk)
        kt = k[:, c].T
        out.append(
            pack(jnp.concatenate([gq_map[c, :], nn(kt, z2[0]) + nn(kt, z2[1])], 1))
        )
    send[...] = jnp.concatenate(out, 0).reshape(chips, rows, LANES)


def sixth_kernel(got, wk, kh, kl, gvl, dz, _, whole):
    rows = WIDE // got.shape[0]
    later = got[:, :rows, :].reshape(WIDE, LANES)
    for p in range(PAIRS):
        c = cols(p)
        w = cols(p, 2 * LANES)
        whole[:, c] = both(nt, split(dz[:, c]), wk[c])
        grad = gvl[:, c] + three(nt, (kh[:, w], kl[:, w]), split(unpack(later[c])))
        whole[:, WIDE + p * LANES : WIDE + (p + 1) * LANES] = grad


def theirs_kernel(first, second, send):
    rows = pl.ds(pl.multiple_of((1 - core()) * TOK, TOK), TOK)
    send[:, :WIDE] = first[rows, :]
    send[:, WIDE:] = second[rows, :]


def finish_kernel(first, second, got, *outs):
    *outs, token = outs
    token[...] = jnp.zeros_like(token)
    rows = pl.ds(pl.multiple_of(core() * TOK, TOK), TOK)
    own = jnp.concatenate([first[rows, :], second[rows, :]], 1)
    other = got[1 - core()]
    zero = core() == 0
    for i, out in enumerate(outs):
        lanes = slice(i * WIDE, (i + 1) * WIDE)
        a, b = own[:, lanes], other[:, lanes]
        out[:, :WIDE] = jnp.where(zero, a, b).astype(BF16)
        out[:, WIDE:] = jnp.where(zero, b, a).astype(BF16)


def sum_kernel(got, *rest):
    send = rest[-1]
    total = got[0]
    for m in range(1, got.shape[0]):
        total = total + got[m]
    send[...] = jnp.broadcast_to(total[None], send.shape)


def sum_cores_kernel(got, _, send):
    acc = [got[0], got[1]]
    for m in range(2, got.shape[0]):
        acc[m % 2] = acc[m % 2] + got[m]
    send[...] = jnp.broadcast_to(jnp.concatenate(acc, 0)[None], send.shape)


def last_kernel(scale, got, gq, gk):
    rows = got.shape[1] // 2
    cores = [got[:, :rows, :].reshape(WIDE, LANES), got[:, rows:, :].reshape(WIDE, LANES)]
    for p in range(2 * PAIRS):
        x = cores[p // PAIRS][cols(p % PAIRS), :] * scale
        y = pltpu.roll(x, HALF, 1)
        gq[2 * p] = x[:HALF, :HALF].astype(BF16)
        gq[2 * p + 1] = y[HALF:, :HALF].astype(BF16)
        gk[2 * p] = x[HALF:, :HALF].astype(BF16)
        gk[2 * p + 1] = y[:HALF, :HALF].astype(BF16)


def call(kernel, outs, *args, flops=10**8, space=pltpu.VMEM, scratch=(), room=32):
    shapes = [jax.ShapeDtypeStruct(shape, dtype) for shape, dtype in outs]
    moved = sum(a.size * a.dtype.itemsize for a in (*args, *shapes))
    return pl.pallas_call(
        kernel,
        out_shape=shapes,
        in_specs=[pl.BlockSpec(memory_space=space)] * len(args),
        out_specs=[pl.BlockSpec(memory_space=pltpu.VMEM)] * len(outs),
        scratch_shapes=scratch,
        compiler_params=pltpu.CompilerParams(vmem_limit_bytes=int(room * 2**20)),
        cost_estimate=pl.CostEstimate(flops=flops, bytes_accessed=moved, transcendentals=0),
    )(*args)


def per_device(sizes, queries, keys, values, upstream, query_map, key_map):
    chips = sizes["z"] * sizes["x"]
    rows = WIDE // chips
    q, k, v, g = (a.reshape(TOK, 2 * WIDE) for a in (queries, keys, values, upstream))
    qmap = query_map.reshape(2 * WIDE, HALF)
    kmap = key_map.reshape(2 * WIDE, HALF)
    feats = ((BLOCK, 2 * WIDE), BF16)
    feats32 = ((BLOCK, 2 * WIDE), F32)
    flat = ((BLOCK, WIDE), F32)
    small = ((BLOCK, WIDE), BF16)
    sums = ((8, LANES), F32)

    def across(a):
        return lax.all_gather(a, "core")

    def exchange(a):
        return lax.all_to_all(a, CHIPS, 0, 0)

    def start(a, b, maps, room):
        send, own, wide = call(
            start_kernel,
            [((TOK, 2 * WIDE), F32), ((TOK, 2 * WIDE), BF16), ((WIDE, LANES), BF16)],
            a, b, maps,
            space=pl.ANY,
            room=room,
            scratch=[
                pltpu.VMEM((TOK, 2 * WIDE), BF16),
                pltpu.VMEM((WIDE, HALF), BF16),
                pltpu.SemaphoreType.DMA((5,)),
            ],
        )
        return own, across(send), wide

    own, got, wk = start(k, v, kmap, 60)
    send, k2, v2, kh, kl = call(
        keys_kernel, [((chips, rows + 8, LANES), F32), small, small, feats, feats], own, got, wk
    )
    first = exchange(send)
    own, got, wq = start(q, g, qmap, 32)
    q2, g2, qh, ql, numl, denl = call(
        queries_kernel,
        [small, small, feats, feats, flat, flat],
        own, got, wq, v2, kh, kl,
        flops=10**9,
    )
    send, den, dn, ksum = call(
        functools.partial(second_kernel, sizes),
        [((chips, 2 * rows, LANES), F32), flat, flat, sums],
        first, g2, qh, ql, denl,
    )
    second = exchange(send)
    gql, gvl, token = call(
        local_kernel, [feats32, flat, sums], v2, qh, ql, kh, kl, dn, flops=10**9
    )
    send, dd = call(
        third_kernel,
        [((chips, rows + 8, LANES), F32), flat],
        second, g2, qh, ql, numl, den, token,
    )
    third = exchange(send)
    whole_q, gq_map, gkl = call(
        fourth_kernel,
        [flat, ((WIDE, LANES), F32), feats32],
        second, q2, v2, wq, qh, ql, kh, kl, dn, dd, ksum, gql,
        flops=10**9,
    )
    send, dz = call(
        functools.partial(fifth_kernel, sizes),
        [((chips, rows, LANES), F32), flat],
        third, k2, v2, kh, kl, gkl, gq_map,
    )
    got = exchange(send)
    others = sizes["dp"] * sizes["core"]
    (partial,) = call(sum_kernel, [((others, rows, LANES), F32)], got)
    (whole,) = call(
        sixth_kernel,
        [((BLOCK, 2 * WIDE), F32)],
        third, wk, kh, kl, gvl, dz, partial,
        flops=10**9,
    )
    (send,) = call(theirs_kernel, [((TOK, 3 * WIDE), F32)], whole_q, whole)
    outs = [((TOK, 2 * WIDE), BF16)] * 3
    grad_q, grad_k, grad_v, token = call(
        finish_kernel, outs + [sums], whole_q, whole, across(send)
    )
    got = lax.all_to_all(partial, ("dp", "core"), 0, 0)
    (send,) = call(sum_cores_kernel, [((chips, 2 * rows, LANES), F32)], got, token)
    got = exchange(send)
    scale = float(BLOCK * chips * sizes["dp"]) ** (-0.5)
    heads = ((8, HALF, HALF), BF16)
    total_q, total_k = call(
        functools.partial(last_kernel, scale), [heads, heads], got
    )
    shape = queries.shape
    return grad_q.reshape(shape), grad_k.reshape(shape), grad_v.reshape(shape), total_q, total_k


def physical(mesh):
    dp, ctx = mesh.devices.shape
    x = 4 if ctx % 8 == 0 and ctx > 8 else 2
    sizes = {"dp": dp, "z": ctx // (2 * x), "x": x, "core": 2}
    return Mesh(mesh.devices.reshape(tuple(sizes.values())), tuple(sizes)), sizes


def solution(mesh):
    inner, sizes = physical(mesh)
    tokens = P("dp", CTX, None)
    return jax.shard_map(
        functools.partial(per_device, sizes),
        mesh=inner,
        in_specs=(tokens,) * 4 + (P(), P()),
        out_specs=(tokens,) * 3 + (P(), P()),
        check_vma=False,
    )
```
